32 devices in a mesh: dom: 8 (over y, x, core), grp: 4 (over z).
Axes of the slice: x: 2, y: 2, z: 4, core: 2. Of those that a mesh axis runs over, the one named last changes fastest.
Arguments:
- positions: float32 [3, 16384], P(None, ('dom', 'grp')), may hold values from -6 to 6
- mass: float32 [16384], P(('dom', 'grp')), may hold values from 0.05 to 0.2
- smooth: float32 [16384], P(('dom', 'grp')), may hold values from 1.5 to 3.5
- counts: int32 [64], P(('dom', 'grp')), may hold values from 128 to 256
- tasks: int32 [2, 128], P(None, ('dom', 'grp')), may hold values from 0 to 23, as said below
Outputs:
- density: float32 [16384], P(('dom', 'grp'))
- accel: float32 [3, 16384], P(None, ('dom', 'grp'))
The draws below stay inside these ranges and needn't reach their ends.
Inputs may be any that keep to these rules, and one draw needn't show every extreme that they name: In every slab, for each b the slab's tasks whose receiving cell lies among slab cells b * 2 to (b + 1) * 2 - 1 number at most 12, and exactly 12 for one b; a cell may receive no task.
All inputs are finite; a program needn't handle non-finite values.
Results may differ from the reference program's by a relative error of at most 0.00017.
Values sent between devices are 32-bit elements; how exact they have to be, the bound alone decides.
A program may use at most 64 MiB of HBM per device.

```python
import math
import jax
import jax.numpy as jnp
from jax import lax

CELL = 256
CD = 2
PT = 4
OCAP = 12
CELLS = 64
TASKS = 128
PARTICLES = 16384
N_DOM = 8
N_GRP = 4


def slab_receivers(single):
    busy_key = jax.random.fold_in(single, 3)
    cell_key = jax.random.fold_in(single, 5)
    perm_key = jax.random.fold_in(single, 7)
    total = N_GRP * PT
    busy = jax.random.randint(busy_key, (), 0, N_GRP)
    ranks = jnp.arange(total, dtype=jnp.int32)
    others = jnp.maximum(ranks - OCAP, 0) % (N_GRP - 1)
    others = jnp.where(others >= busy, others + 1, others)
    blocks = jnp.where(ranks < OCAP, busy, others)
    inner = jax.random.randint(cell_key, (total,), 0, CD)
    receivers = (blocks * CD + inner).astype(jnp.int32)
    shuffle = jax.random.permutation(perm_key, total)
    return receivers[shuffle]


def draw_tasks(key, part):
    first_key = jax.random.fold_in(key, 11)
    second_key = jax.random.fold_in(key, 23)
    slab_cells = N_GRP * CD
    keys = jax.random.split(first_key, N_DOM)
    receivers = jax.vmap(slab_receivers)(keys).reshape(TASKS).astype(jnp.int32)
    sources = jax.random.randint(second_key, (TASKS,), 0, 3 * slab_cells).astype(jnp.int32)
    return jnp.stack([receivers, sources], 0)


def plant(array, own_key, low, largest):
    dims = array.shape
    place = [jax.random.randint(jax.random.fold_in(own_key, axis), (), 0, dims[axis]) for axis in range(len(dims))]
    array = array.at[tuple(place)].set(low)
    longest = dims.index(max(dims))
    place[longest] = (place[longest] + 1) % dims[longest]
    return array.at[tuple(place)].set(largest)


def level_of(stream_key, dims, pieces, smallest, high):
    level, own = 1.0, jax.random.fold_in(stream_key, 6)
    for dim, blocks in pieces:
        heights = jnp.exp(jax.random.uniform(jax.random.fold_in(own, dim), (blocks,), jnp.float32, smallest / len(pieces), high / len(pieces)))
        level = level * jnp.repeat(heights, dims[dim] // blocks).reshape([-1 if axis == dim else 1 for axis in range(len(dims))])
    return level


def normal_values(own_key, dims, scale, bound, cuts=(), held_as=jnp.bfloat16):
    array = jax.random.normal(own_key, dims, jnp.float32) * scale
    if len(cuts) > 0:
        array = level_of(own_key, dims, cuts, -0.22, 0.18) * array
    return jnp.clip(array, min=-bound, max=bound).astype(held_as)


def setup_inputs(seed: int = 0) -> dict:
    arg_keys = jax.random.split(jax.random.key(seed), 6)
    positions = normal_values(arg_keys[0], (3, PARTICLES), 1.0, 6.0, ((1, 32),), jnp.float32)
    mass = jnp.clip(jnp.exp(math.log(0.2) - 1.3862944 * jax.random.uniform(arg_keys[1], (PARTICLES,), jnp.float32) ** level_of(arg_keys[1], (PARTICLES,), ((0, 32),), -0.2, 0.2)), 0.05, 0.2)
    smooth = jnp.clip(jnp.exp(math.log(3.5) - 0.84729786 * jax.random.uniform(arg_keys[2], (PARTICLES,), jnp.float32) ** level_of(arg_keys[2], (PARTICLES,), ((0, 32),), -0.2, 0.2)), 1.5, 3.5)
    counts = plant(jax.random.randint(arg_keys[3], (CELLS,), 128, 257), jax.random.fold_in(arg_keys[3], 1), 128, 256).astype(jnp.int32)
    tasks = draw_tasks(jax.random.fold_in(arg_keys[5], 71), 0)
    return dict(positions=positions, mass=mass, smooth=smooth, counts=counts, tasks=tasks)


def tile_terms(recv, source):
    diff_x = recv[0][:, None] - source[0][None, :]
    diff_y = recv[1][:, None] - source[1][None, :]
    diff_z = recv[2][:, None] - source[2][None, :]
    radius = jnp.sqrt(diff_x * diff_x + diff_y * diff_y + diff_z * diff_z)
    length = recv[4][:, None]
    inside = jnp.maximum(1.0 - radius / length, 0.0)
    return (diff_x, diff_y, diff_z, radius, length, inside)

def density_tile(recv, source):
    diff_x, diff_y, diff_z, radius, length, inside = tile_terms(recv, source)
    weight = inside ** 4 * (1.0 + 4.0 * radius / length) * (21.0 / (2.0 * math.pi)) / length ** 3
    return lax.optimization_barrier(jnp.sum(weight * source[3][None, :], axis=1))

def force_tile(recv, source, rho_recv, rho_source):
    diff_x, diff_y, diff_z, radius, length, inside = tile_terms(recv, source)
    coeff = source[3][None, :] * (1.0 / rho_recv[:, None] + 1.0 / rho_source[None, :])
    coeff = coeff * inside ** 3 * (105.0 / math.pi) / length ** 5
    return jnp.stack([lax.optimization_barrier(jnp.sum(coeff * diff_x, 1)), lax.optimization_barrier(jnp.sum(coeff * diff_y, 1)), lax.optimization_barrier(jnp.sum(coeff * diff_z, 1))], 0)

def reference(positions, mass, smooth, counts, tasks):
    cells = counts.shape[0]
    live = (jnp.arange(CELL, dtype=jnp.int32)[None, :] < counts[:, None]).astype(jnp.float32)
    mass_cells = mass.reshape(cells, CELL)
    smooth_cells = smooth.reshape(cells, CELL)
    packed = jnp.concatenate([positions.reshape(3, cells, CELL), (mass_cells * live)[None], smooth_cells[None]], 0)
    slab_cells = N_GRP * CD
    order = jnp.arange(TASKS, dtype=jnp.int32)
    slab_of = order // (N_GRP * PT)
    recv_cell = (slab_of * slab_cells + tasks[0]).astype(jnp.int32)
    side = tasks[1] // slab_cells
    source_cell = ((slab_of + side - 1) % N_DOM * slab_cells + tasks[1] % slab_cells).astype(jnp.int32)

    def dens(pair):
        return density_tile(packed[:, pair[0]], packed[:, pair[1]])
    partial_value = lax.map(dens, (recv_cell, source_cell), batch_size=64)
    self_term = mass_cells * (21.0 / (2.0 * math.pi)) / smooth_cells ** 3
    rho = self_term + jax.ops.segment_sum(partial_value, recv_cell, num_segments=cells)

    def force(pair):
        return force_tile(packed[:, pair[0]], packed[:, pair[1]], rho[pair[0]], rho[pair[1]])
    force_part = lax.map(force, (recv_cell, source_cell), batch_size=64)
    accel = jax.ops.segment_sum(force_part, recv_cell, num_segments=cells)
    accel = jnp.transpose(accel * live[:, None, :], (1, 0, 2)).reshape(3, cells * CELL)
    density = (rho * live).reshape(cells * CELL)
    return (density, accel)
```

```python
import functools
import math

import jax
import jax.numpy as jnp
from jax import lax
from jax.experimental import pallas as pl
from jax.experimental.pallas import tpu as pltpu
from jax.sharding import PartitionSpec as P

CELL = 256
LANES = 128
HALVES = CELL // LANES
CHUNK = 32
MESH = pl.DeviceIdType.MESH
DENSITY_SCALE = 21.0 / (2.0 * math.pi)
FORCE_SCALE = 105.0 / math.pi


def kernel(
    doms, groups, pairs, tasks_ref, counts_ref, pos_ref, mass_ref, smooth_ref,
    rho_out, acc_out,
    pool, parts, rho, tasks_v, tasks_s, send_sem, recv_sem, psend_sem, precv_sem, tsend_sem, trecv_sem, local_sem,
):
    cells = counts_ref.shape[0]
    slab_cells = groups * cells
    dom = lax.axis_index("dom")
    member = lax.axis_index("grp")
    own = groups + member
    peers = [(e, g) for e in (0, -1, 1) for g in range(groups) if not (e == 0 and g == 0)]

    def place(e, g):
        return (lax.rem(dom + e + doms, doms), lax.rem(member + g, groups))

    barrier = pltpu.get_barrier_semaphore()
    for e, g in peers:
        pl.semaphore_signal(barrier, inc=1, device_id=place(e, g), device_id_type=MESH)

    lane = lax.broadcasted_iota(jnp.int32, (1, LANES), 1)
    for c in range(cells):
        for h in range(HALVES):
            at = pl.ds(c * CELL + h * LANES, LANES)
            live = (lane + h * LANES < counts_ref[c]).astype(jnp.float32)
            for d in range(3):
                pool[own, c, pl.ds(d * HALVES + h, 1), :] = pos_ref[pl.ds(d, 1), at]
            pool[own, c, pl.ds(3 * HALVES + h, 1), :] = mass_ref[:, at] * live
            pool[own, cells, pl.ds(c * HALVES + h, 1), :] = smooth_ref[:, at]
    row = jnp.zeros((1, LANES), jnp.int32)
    for t in range(pairs):
        pool[own, cells, pl.ds(cells * HALVES + t, 1), :] = jnp.full((1, LANES), tasks_ref[0, t]).astype(jnp.float32)
        row = jnp.where(lane == t, tasks_ref[0, t], row)
        row = jnp.where(lane == pairs + t, tasks_ref[1, t], row)
    tasks_v[member] = row

    def exchange(ref, sends, recvs, e, g, n):
        slot = (1 - e) * groups + member
        return pltpu.make_async_remote_copy(
            src_ref=ref.at[own], dst_ref=ref.at[slot], send_sem=sends.at[n], recv_sem=recvs.at[slot],
            device_id=place(e, g), device_id_type=MESH,
        )

    def arrival(ref, sends, recvs, e, g):
        slot = (1 + e) * groups + lax.rem(member + g, groups)
        return pltpu.make_async_remote_copy(
            src_ref=ref.at[own], dst_ref=ref.at[slot], send_sem=sends.at[0], recv_sem=recvs.at[slot],
            device_id=place(e, g), device_id_type=MESH,
        )

    pl.semaphore_wait(barrier, len(peers))
    first = [exchange(pool, send_sem, recv_sem, e, g, n) for n, (e, g) in enumerate(peers)]
    for copy in first:
        copy.start()
    lists = []
    for g in range(1, groups):
        copy = pltpu.make_async_remote_copy(
            src_ref=tasks_v.at[member], dst_ref=tasks_v.at[member], send_sem=tsend_sem.at[g],
            recv_sem=trecv_sem.at[member], device_id=place(0, g), device_id_type=MESH,
        )
        copy.start()
        lists.append(copy)
    for g in range(1, groups):
        other = lax.rem(member + g, groups)
        pltpu.make_async_remote_copy(
            src_ref=tasks_v.at[member], dst_ref=tasks_v.at[other], send_sem=tsend_sem.at[0],
            recv_sem=trecv_sem.at[other], device_id=place(0, g), device_id_type=MESH,
        ).wait_recv()
    to_scalar = pltpu.make_async_copy(tasks_v, tasks_s, local_sem)
    to_scalar.start()
    for e, g in peers:
        arrival(pool, send_sem, recv_sem, e, g).wait_recv()

    def receiver(slot, cell):
        block = pool[slot, cell]
        rest = pool[slot, cells]
        length = rest[0:HALVES]
        for c in range(1, cells):
            length = jnp.where(cell == c, rest[c * HALVES:(c + 1) * HALVES], length)
        inverse = 1.0 / length
        rows = []
        for h in range(HALVES):
            rows.append([block[d * HALVES + h:d * HALVES + h + 1] for d in range(3)] + [inverse[h:h + 1]])
        return rows

    def chunks(source):
        for s in range(HALVES):
            for q in range(0, LANES, CHUNK):
                yield s, q, [source[q:q + CHUNK, d * HALVES + s:d * HALVES + s + 1] for d in range(4)]

    def inside(row, col):
        diffs = [row[d] - col[d] for d in range(3)]
        square = (diffs[0] * diffs[0] + diffs[1] * diffs[1] + diffs[2] * diffs[2]) * (row[3] * row[3])
        ratio = square * lax.rsqrt(jnp.maximum(square, 1e-30))
        return diffs, jnp.maximum(1.0 - ratio, 0.0)

    def density(t, carry):
        recv, k = tasks_ref[0, t], tasks_ref[1, t]
        rows = receiver(groups + recv // cells, lax.rem(recv, cells))
        source = jnp.transpose(pool[k // cells, lax.rem(k, cells)])
        total = [jnp.zeros((CHUNK, LANES), jnp.float32) for _ in range(HALVES)]
        for s, q, col in chunks(source):
            for h in range(HALVES):
                _, u = inside(rows[h], col)
                u2 = u * u
                total[h] = total[h] + (u2 * u2) * (5.0 - 4.0 * u) * col[3]
        for h in range(HALVES):
            value = jnp.sum(total[h], axis=0, keepdims=True)
            inv = rows[h][3]
            parts[own, pl.ds(t * HALVES + h, 1), :] = value * (inv * inv * inv) * DENSITY_SCALE
        return carry

    lax.fori_loop(0, pairs, density, 0)
    second = [exchange(parts, psend_sem, precv_sem, e, g, n) for n, (e, g) in enumerate(peers)]
    for copy in second:
        copy.start()

    for slot in range(3 * groups):
        for c in range(cells):
            m = pool[slot, c, pl.ds(3 * HALVES, HALVES), :]
            inv = 1.0 / pool[slot, cells, pl.ds(c * HALVES, HALVES), :]
            rho[pl.ds((slot * cells + c) * HALVES, HALVES), :] = m * (inv * inv * inv) * DENSITY_SCALE
    to_scalar.wait()

    for e, g in peers:
        arrival(parts, psend_sem, precv_sem, e, g).wait_recv()

    span = slab_cells * HALVES
    index = lax.broadcasted_iota(jnp.int32, (span, LANES), 0)
    odd = lax.rem(index, HALVES)
    cell_of = (index // HALVES).astype(jnp.float32)
    for d in range(3):
        total = rho[pl.ds(d * span, span), :]
        for g in range(groups):
            slot = d * groups + g
            part = parts[slot]
            to = pool[slot, cells]
            for t in range(pairs):
                value = part[t * HALVES:t * HALVES + 1]
                for h in range(1, HALVES):
                    value = jnp.where(odd == h, part[t * HALVES + h:t * HALVES + h + 1], value)
                at = to[cells * HALVES + t:cells * HALVES + t + 1]
                total = total + jnp.where(cell_of == at, value, 0.0)
        rho[pl.ds(d * span, span), :] = total

    for c in range(cells):
        for h in range(HALVES):
            rho_out[pl.ds(c * HALVES + h, 1), :] = rho[pl.ds((own * cells + c) * HALVES + h, 1), :]
    acc_out[...] = jnp.zeros_like(acc_out)

    def force(t, carry):
        j, i = t // pairs, lax.rem(t, pairs)
        recv, k = tasks_s[j, 0, i], tasks_s[j, 0, pairs + i]
        cell = lax.rem(recv, cells)
        mine = recv // cells == member
        rows = receiver(own, cell)
        block = pool[k // cells, lax.rem(k, cells)]
        k_rho = rho[pl.ds(k * HALVES, HALVES), :]
        weight = block[3 * HALVES:4 * HALVES] / jnp.maximum(k_rho, 1e-30)
        source = jnp.transpose(block)
        heavy = jnp.transpose(jnp.concatenate([weight] * (8 // HALVES), axis=0))
        a_rho = 1.0 / jnp.maximum(rho[pl.ds((own * cells + cell) * HALVES, HALVES), :], 1e-30)
        total = [[jnp.zeros((CHUNK, LANES), jnp.float32) for _ in range(3)] for _ in range(HALVES)]
        for s, q, col in chunks(source):
            ratio = heavy[q:q + CHUNK, s:s + 1]
            for h in range(HALVES):
                diffs, u = inside(rows[h], col)
                coeff = (u * u) * u * (col[3] * a_rho[h:h + 1] + ratio)
                for d in range(3):
                    total[h][d] = total[h][d] + coeff * diffs[d]
        for h in range(HALVES):
            inv = rows[h][3]
            fifth = FORCE_SCALE * (inv * inv) * (inv * inv) * inv
            for d in range(3):
                value = jnp.sum(total[h][d], axis=0, keepdims=True) * fifth
                for c in range(cells):
                    at = pl.ds((d * cells + c) * HALVES + h, 1)
                    acc_out[at, :] += jnp.where(jnp.logical_and(mine, cell == c), value, 0.0)
        return carry

    lax.fori_loop(0, groups * pairs, force, 0)
    for c in range(cells):
        for h in range(HALVES):
            live = (lane + h * LANES < counts_ref[c]).astype(jnp.float32)
            at = pl.ds(c * HALVES + h, 1)
            rho_out[at, :] = rho_out[at, :] * live
            for d in range(3):
                at = pl.ds((d * cells + c) * HALVES + h, 1)
                acc_out[at, :] = acc_out[at, :] * live

    for copy in first + lists + second:
        copy.wait_send()


def local(positions, mass, smooth, counts, tasks):
    groups, doms = lax.axis_size("grp"), lax.axis_size("dom")
    cells, pairs = counts.shape[0], tasks.shape[1]
    around = 3 * groups
    last = max(8, -(-(cells * HALVES + pairs) // 8) * 8)
    vmem, smem = (pl.BlockSpec(memory_space=space) for space in (pltpu.VMEM, pltpu.SMEM))
    density, accel = pl.pallas_call(
        functools.partial(kernel, doms, groups, pairs),
        out_shape=(
            jax.ShapeDtypeStruct((cells * HALVES, LANES), jnp.float32),
            jax.ShapeDtypeStruct((3 * cells * HALVES, LANES), jnp.float32),
        ),
        in_specs=[smem, smem, vmem, vmem, vmem],
        out_specs=(vmem, vmem),
        scratch_shapes=[
            pltpu.VMEM((around, cells + 1, last, LANES), jnp.float32),
            pltpu.VMEM((around, pairs * HALVES, LANES), jnp.float32),
            pltpu.VMEM((around * cells * HALVES, LANES), jnp.float32),
            pltpu.VMEM((groups, 1, LANES), jnp.int32),
            pltpu.SMEM((groups, 1, LANES), jnp.int32),
            pltpu.SemaphoreType.DMA((around,)),
            pltpu.SemaphoreType.DMA((around,)),
            pltpu.SemaphoreType.DMA((around,)),
            pltpu.SemaphoreType.DMA((around,)),
            pltpu.SemaphoreType.DMA((groups,)),
            pltpu.SemaphoreType.DMA((groups,)),
            pltpu.SemaphoreType.DMA,
        ],
        compiler_params=pltpu.CompilerParams(
            collective_id=0, has_side_effects=True, vmem_limit_bytes=48 * 1024 * 1024
        ),
    )(tasks, counts, positions, mass[None], smooth[None])
    return density.reshape(-1), accel.reshape(3, -1)


def solution(mesh):
    in_specs = (
        P(None, ("dom", "grp")),
        P(("dom", "grp")),
        P(("dom", "grp")),
        P(("dom", "grp")),
        P(None, ("dom", "grp")),
    )
    out_specs = (P(("dom", "grp")), P(None, ("dom", "grp")))
    return jax.shard_map(local, mesh=mesh, in_specs=in_specs, out_specs=out_specs, check_vma=False)
```

```python
import functools
import math

import jax
import jax.numpy as jnp
from jax import lax
from jax.experimental import pallas as pl
from jax.experimental.pallas import tpu as pltpu
from jax.sharding import PartitionSpec as P

CELL = 256
LANES = 128
HALVES = CELL // LANES
CHUNK = 32
MESH = pl.DeviceIdType.MESH
DENSITY_SCALE = 21.0 / (2.0 * math.pi)
FORCE_SCALE = 105.0 / math.pi


def kernel(
    doms, groups, cells, pairs, tasks_hbm, counts_hbm, pos_hbm, mass_hbm, smooth_hbm,
    rho_out, acc_out,
    tasks_ref, counts_ref, pos_ref, mass_ref, smooth_ref,
    pool, parts, rho, forces, waiting, early,
    in_sem, send_sem, recv_sem, psend_sem, precv_sem, fsend_sem, frecv_sem,
):
    slab_cells = groups * cells
    dom = lax.axis_index("dom")
    member = lax.axis_index("grp")
    own = groups + member
    peers = [(e, g) for e in (0, -1, 1) for g in range(groups) if not (e == 0 and g == 0)]

    def place(e, g):
        return (lax.rem(dom + e + doms, doms), lax.rem(member + g, groups))

    barrier = pltpu.get_barrier_semaphore()
    for e, g in peers:
        pl.semaphore_signal(barrier, inc=1, device_id=place(e, g), device_id_type=MESH)
    moves = (
        (tasks_hbm, tasks_ref), (counts_hbm, counts_ref), (pos_hbm, pos_ref), (mass_hbm, mass_ref),
        (smooth_hbm, smooth_ref),
    )
    inputs = [pltpu.make_async_copy(*move, in_sem.at[n]) for n, move in enumerate(moves)]
    for copy in inputs:
        copy.start()
    for copy in inputs:
        copy.wait()

    lane = lax.broadcasted_iota(jnp.int32, (1, LANES), 1)
    for c in range(cells):
        for h in range(HALVES):
            at = pl.ds(c * CELL + h * LANES, LANES)
            live = (lane + h * LANES < counts_ref[c]).astype(jnp.float32)
            for d in range(3):
                pool[own, c, pl.ds(d * HALVES + h, 1), :] = pos_ref[pl.ds(d, 1), at]
            pool[own, c, pl.ds(3 * HALVES + h, 1), :] = mass_ref[:, at] * live
            pool[own, cells, pl.ds(c * HALVES + h, 1), :] = smooth_ref[:, at]
    for t in range(pairs):
        pool[own, cells, pl.ds(cells * HALVES + t, 1), :] = jnp.full((1, LANES), tasks_ref[0, t]).astype(jnp.float32)

    def exchange(ref, sends, recvs, e, g, n):
        slot = (1 - e) * groups + member
        return pltpu.make_async_remote_copy(
            src_ref=ref.at[own], dst_ref=ref.at[slot], send_sem=sends.at[n], recv_sem=recvs.at[slot],
            device_id=place(e, g), device_id_type=MESH,
        )

    def arrival(ref, sends, recvs, e, g):
        slot = (1 + e) * groups + lax.rem(member + g, groups)
        return pltpu.make_async_remote_copy(
            src_ref=ref.at[own], dst_ref=ref.at[slot], send_sem=sends.at[0], recv_sem=recvs.at[slot],
            device_id=place(e, g), device_id_type=MESH,
        )

    pl.semaphore_wait(barrier, len(peers))
    first = [exchange(pool, send_sem, recv_sem, e, g, n) for n, (e, g) in enumerate(peers)]
    for copy in first:
        copy.start()
    for e, g in peers:
        arrival(pool, send_sem, recv_sem, e, g).wait_recv()

    def receiver(slot, cell):
        block = pool[slot, cell]
        rest = pool[slot, cells]
        length = rest[0:HALVES]
        for c in range(1, cells):
            length = jnp.where(cell == c, rest[c * HALVES:(c + 1) * HALVES], length)
        inverse = 1.0 / length
        rows = []
        for h in range(HALVES):
            rows.append([block[d * HALVES + h:d * HALVES + h + 1] for d in range(3)] + [inverse[h:h + 1]])
        return rows

    def chunks(source):
        for s in range(HALVES):
            for q in range(0, LANES, CHUNK):
                yield s, q, [source[q:q + CHUNK, d * HALVES + s:d * HALVES + s + 1] for d in range(4)]

    def inside(row, col):
        diffs = [row[d] - col[d] for d in range(3)]
        square = (diffs[0] * diffs[0] + diffs[1] * diffs[1] + diffs[2] * diffs[2]) * (row[3] * row[3])
        ratio = square * lax.rsqrt(jnp.maximum(square, 1e-30))
        return diffs, jnp.maximum(1.0 - ratio, 0.0)

    def task(t):
        recv, k = tasks_ref[0, t], tasks_ref[1, t]
        rows = receiver(groups + recv // cells, lax.rem(recv, cells))
        return rows, jnp.transpose(pool[k // cells, lax.rem(k, cells)])

    def density(t, carry):
        rows, source = task(t)
        total = [jnp.zeros((CHUNK, LANES), jnp.float32) for _ in range(HALVES)]
        for s, q, col in chunks(source):
            for h in range(HALVES):
                _, u = inside(rows[h], col)
                u2 = u * u
                total[h] = total[h] + (u2 * u2) * (5.0 - 4.0 * u) * col[3]
        for h in range(HALVES):
            value = jnp.sum(total[h], axis=0, keepdims=True)
            inv = rows[h][3]
            parts[own, pl.ds(t * HALVES + h, 1), :] = value * (inv * inv * inv) * DENSITY_SCALE
        return carry

    lax.fori_loop(0, pairs, density, 0)
    second = [exchange(parts, psend_sem, precv_sem, e, g, n) for n, (e, g) in enumerate(peers)]
    for copy in second:
        copy.start()

    def prepare(t, carry):
        rows, source = task(t)
        total = [[jnp.zeros((CHUNK, LANES), jnp.float32) for _ in range(3)] for _ in range(HALVES)]
        for s, q, col in chunks(source):
            for h in range(HALVES):
                diffs, u = inside(rows[h], col)
                coeff = (u * u) * u * col[3]
                for d in range(3):
                    term = coeff * diffs[d]
                    waiting[t, d * HALVES + h, pl.ds(s * LANES + q, CHUNK), :] = term
                    total[h][d] = total[h][d] + term
        for h in range(HALVES):
            inv = rows[h][3]
            early[t, pl.ds(3 * HALVES + h, 1), :] = FORCE_SCALE * (inv * inv) * (inv * inv) * inv
            for d in range(3):
                early[t, pl.ds(d * HALVES + h, 1), :] = jnp.sum(total[h][d], axis=0, keepdims=True)
        return carry

    lax.fori_loop(0, pairs, prepare, 0)

    for slot in range(3 * groups):
        for c in range(cells):
            m = pool[slot, c, pl.ds(3 * HALVES, HALVES), :]
            inv = 1.0 / pool[slot, cells, pl.ds(c * HALVES, HALVES), :]
            rho[pl.ds((slot * cells + c) * HALVES, HALVES), :] = m * (inv * inv * inv) * DENSITY_SCALE

    for e, g in peers:
        arrival(parts, psend_sem, precv_sem, e, g).wait_recv()

    span = slab_cells * HALVES
    index = lax.broadcasted_iota(jnp.int32, (span, LANES), 0)
    odd = lax.rem(index, HALVES)
    cell_of = (index // HALVES).astype(jnp.float32)
    for d in range(3):
        total = rho[pl.ds(d * span, span), :]
        for g in range(groups):
            slot = d * groups + g
            part = parts[slot]
            to = pool[slot, cells]
            for t in range(pairs):
                value = part[t * HALVES:t * HALVES + 1]
                for h in range(1, HALVES):
                    value = jnp.where(odd == h, part[t * HALVES + h:t * HALVES + h + 1], value)
                at = to[cells * HALVES + t:cells * HALVES + t + 1]
                total = total + jnp.where(cell_of == at, value, 0.0)
        rho[pl.ds(d * span, span), :] = total

    source_rho = [rho[pl.ds(tasks_ref[1, t] * HALVES, HALVES), :] for t in range(pairs)]
    source_rho = 1.0 / jnp.maximum(jnp.concatenate(source_rho, axis=0), 1e-30)
    columns = jnp.transpose(source_rho)
    for t in range(pairs):
        recv = tasks_ref[0, t]
        a_rho = 1.0 / jnp.maximum(rho[pl.ds((slab_cells + recv) * HALVES, HALVES), :], 1e-30)
        total = [[jnp.zeros((CHUNK, LANES), jnp.float32) for _ in range(3)] for _ in range(HALVES)]
        for s in range(HALVES):
            for q in range(0, LANES, CHUNK):
                col = columns[q:q + CHUNK, t * HALVES + s:t * HALVES + s + 1]
                for h in range(HALVES):
                    for d in range(3):
                        term = waiting[t, d * HALVES + h, pl.ds(s * LANES + q, CHUNK), :]
                        total[h][d] = total[h][d] + term * col
        for h in range(HALVES):
            for d in range(3):
                at = pl.ds(d * HALVES + h, 1)
                value = jnp.sum(total[h][d], axis=0, keepdims=True) + early[t, at, :] * a_rho[h:h + 1]
                forces[member, pl.ds((t * 3 + d) * HALVES + h, 1), :] = value * early[t, pl.ds(3 * HALVES + h, 1), :]

    third = []
    for g in range(1, groups):
        copy = pltpu.make_async_remote_copy(
            src_ref=forces.at[member], dst_ref=forces.at[member], send_sem=fsend_sem.at[g],
            recv_sem=frecv_sem.at[member], device_id=place(0, g), device_id_type=MESH,
        )
        copy.start()
        third.append(copy)

    live = []
    for c in range(cells):
        for h in range(HALVES):
            live.append((lane + h * LANES < counts_ref[c]).astype(jnp.float32))
            at = pl.ds(c * HALVES + h, 1)
            rho_out[at, :] = rho[pl.ds((own * cells + c) * HALVES + h, 1), :] * live[-1]

    for copy in first + second:
        copy.wait_send()
    for g in range(1, groups):
        other = lax.rem(member + g, groups)
        pltpu.make_async_remote_copy(
            src_ref=forces.at[member], dst_ref=forces.at[other], send_sem=fsend_sem.at[0],
            recv_sem=frecv_sem.at[other], device_id=place(0, g), device_id_type=MESH,
        ).wait_recv()

    rows = 3 * HALVES
    total = [jnp.zeros((rows, LANES), jnp.float32) for _ in range(cells)]
    base = (member * cells).astype(jnp.float32)
    for g in range(groups):
        to = pool[groups + g, cells]
        for t in range(pairs):
            value = forces[g, pl.ds(t * rows, rows), :]
            at = to[cells * HALVES + t:cells * HALVES + t + 1]
            for c in range(cells):
                total[c] = total[c] + jnp.where(at == base + c, value, 0.0)
    for c in range(cells):
        for h in range(HALVES):
            for d in range(3):
                row = total[c][d * HALVES + h:d * HALVES + h + 1] * live[c * HALVES + h]
                acc_out[pl.ds(d, 1), pl.ds(c * CELL + h * LANES, LANES)] = row

    for copy in third:
        copy.wait_send()


def local(positions, mass, smooth, counts, tasks):
    groups, doms = lax.axis_size("grp"), lax.axis_size("dom")
    cells, pairs = counts.shape[0], tasks.shape[1]
    around = 3 * groups
    last = max(8, -(-(cells * HALVES + pairs) // 8) * 8)
    vmem, hbm = (pl.BlockSpec(memory_space=space) for space in (pltpu.VMEM, pltpu.HBM))
    density, accel = pl.pallas_call(
        functools.partial(kernel, doms, groups, cells, pairs),
        out_shape=(
            jax.ShapeDtypeStruct((cells * HALVES, LANES), jnp.float32),
            jax.ShapeDtypeStruct(positions.shape, jnp.float32),
        ),
        in_specs=[hbm] * 5,
        out_specs=(vmem, vmem),
        scratch_shapes=[
            pltpu.SMEM(tasks.shape, jnp.int32),
            pltpu.SMEM(counts.shape, jnp.int32),
            pltpu.VMEM(positions.shape, jnp.float32),
            pltpu.VMEM((1, mass.shape[0]), jnp.float32),
            pltpu.VMEM((1, smooth.shape[0]), jnp.float32),
            pltpu.VMEM((around, cells + 1, last, LANES), jnp.float32),
            pltpu.VMEM((around, pairs * HALVES, LANES), jnp.float32),
            pltpu.VMEM((around * cells * HALVES, LANES), jnp.float32),
            pltpu.VMEM((groups, pairs * 3 * HALVES, LANES), jnp.float32),
            pltpu.VMEM((pairs, 3 * HALVES, CELL, LANES), jnp.float32),
            pltpu.VMEM((pairs, 4 * HALVES, LANES), jnp.float32),
            pltpu.SemaphoreType.DMA((5,)),
            pltpu.SemaphoreType.DMA((around,)),
            pltpu.SemaphoreType.DMA((around,)),
            pltpu.SemaphoreType.DMA((around,)),
            pltpu.SemaphoreType.DMA((around,)),
            pltpu.SemaphoreType.DMA((groups,)),
            pltpu.SemaphoreType.DMA((groups,)),
        ],
        compiler_params=pltpu.CompilerParams(
            collective_id=0, has_side_effects=True, vmem_limit_bytes=48 * 1024 * 1024
        ),
    )(tasks, counts, positions, mass[None], smooth[None])
    return density.reshape(-1), accel


def solution(mesh):
    in_specs = (
        P(None, ("dom", "grp")),
        P(("dom", "grp")),
        P(("dom", "grp")),
        P(("dom", "grp")),
        P(None, ("dom", "grp")),
    )
    out_specs = (P(("dom", "grp")), P(None, ("dom", "grp")))
    return jax.shard_map(local, mesh=mesh, in_specs=in_specs, out_specs=out_specs, check_vma=False)
```

```python
import functools
import math

import jax
import jax.numpy as jnp
from jax import lax
from jax.experimental import pallas as pl
from jax.experimental.pallas import tpu as pltpu
from jax.sharding import PartitionSpec as P

CELL = 256
LANES = 128
HALVES = CELL // LANES
CHUNK = 32
MESH = pl.DeviceIdType.MESH
DENSITY_SCALE = 21.0 / (2.0 * math.pi)
FORCE_SCALE = 105.0 / math.pi


def kernel(
    doms, groups, cells, pairs, tasks_hbm, counts_hbm, pos_hbm, mass_hbm, smooth_hbm,
    rho_out, acc_out,
    tasks_ref, counts_ref, pos_ref, mass_ref, smooth_ref,
    pool, slab_tail, far_tail, parts, rho, to_owner, forces, waiting, early,
    in_sem, send_sem, recv_sem, tsend_sem, trecv_sem, psend_sem, precv_sem, fsend_sem, frecv_sem,
):
    slab_cells = groups * cells
    dom = lax.axis_index("dom")
    member = lax.axis_index("grp")
    own = groups + member
    near = [(0, g) for g in range(1, groups)]
    far = [(e, g) for g in range(groups) for e in (-1, 1)]
    peers = far + near

    def place(e, g):
        return (lax.rem(dom + e + doms, doms), lax.rem(member + g, groups))

    barrier = pltpu.get_barrier_semaphore()
    for e, g in peers:
        pl.semaphore_signal(barrier, inc=1, device_id=place(e, g), device_id_type=MESH)
    moves = (
        (tasks_hbm, tasks_ref), (counts_hbm, counts_ref), (pos_hbm, pos_ref), (mass_hbm, mass_ref),
        (smooth_hbm, smooth_ref),
    )
    inputs = [pltpu.make_async_copy(*move, in_sem.at[n]) for n, move in enumerate(moves)]
    for copy in inputs:
        copy.start()
    for copy in inputs:
        copy.wait()

    lane = lax.broadcasted_iota(jnp.int32, (1, LANES), 1)
    for c in range(cells):
        for h in range(HALVES):
            at = pl.ds(c * CELL + h * LANES, LANES)
            live = (lane + h * LANES < counts_ref[c]).astype(jnp.float32)
            for d in range(3):
                pool[own, c, pl.ds(d * HALVES + h, 1), :] = pos_ref[pl.ds(d, 1), at]
            pool[own, c, pl.ds(3 * HALVES + h, 1), :] = mass_ref[:, at] * live
            slab_tail[member, pl.ds(c * HALVES + h, 1), :] = smooth_ref[:, at]
    for t in range(pairs):
        slab_tail[member, pl.ds(cells * HALVES + t, 1), :] = jnp.full((1, LANES), tasks_ref[0, t]).astype(jnp.float32)

    def exchange(ref, sends, recvs, e, g, n):
        slot = (1 - e) * groups + member
        return pltpu.make_async_remote_copy(
            src_ref=ref.at[own], dst_ref=ref.at[slot], send_sem=sends.at[n], recv_sem=recvs.at[slot],
            device_id=place(e, g), device_id_type=MESH,
        )

    def arrival(ref, sends, recvs, e, g):
        slot = (1 + e) * groups + lax.rem(member + g, groups)
        return pltpu.make_async_remote_copy(
            src_ref=ref.at[own], dst_ref=ref.at[slot], send_sem=sends.at[0], recv_sem=recvs.at[slot],
            device_id=place(e, g), device_id_type=MESH,
        )

    pl.semaphore_wait(barrier, len(peers))
    first = [exchange(pool, send_sem, recv_sem, e, g, n) for n, (e, g) in enumerate(peers)]

    def tail_copy(e, g, n, sender):
        slot = ((1 - e) if n > 0 else (1 + e)) * groups + sender
        dst = slab_tail.at[sender] if e == 0 else far_tail.at[slot]
        return pltpu.make_async_remote_copy(
            src_ref=slab_tail.at[member], dst_ref=dst, send_sem=tsend_sem.at[n], recv_sem=trecv_sem.at[slot],
            device_id=place(e, g), device_id_type=MESH,
        )

    first += [tail_copy(e, g, n + 1, member) for n, (e, g) in enumerate(near + far)]
    for copy in first:
        copy.start()
    for e, g in peers:
        arrival(pool, send_sem, recv_sem, e, g).wait_recv()
    for e, g in near:
        tail_copy(e, g, 0, lax.rem(member + g, groups)).wait_recv()

    def tail_of(slot):
        return slab_tail.at[slot - groups] if slot // groups == 1 else far_tail.at[slot]

    def receiver(slot, cell):
        block = pool[slot, cell]
        rest = slab_tail[slot - groups]
        length = rest[0:HALVES]
        for c in range(1, cells):
            length = jnp.where(cell == c, rest[c * HALVES:(c + 1) * HALVES], length)
        inverse = 1.0 / length
        rows = []
        for h in range(HALVES):
            rows.append([block[d * HALVES + h:d * HALVES + h + 1] for d in range(3)] + [inverse[h:h + 1]])
        return rows

    def chunks(source):
        for s in range(HALVES):
            for q in range(0, LANES, CHUNK):
                yield s, q, [source[q:q + CHUNK, d * HALVES + s:d * HALVES + s + 1] for d in range(4)]

    def inside(row, col):
        diffs = [row[d] - col[d] for d in range(3)]
        square = (diffs[0] * diffs[0] + diffs[1] * diffs[1] + diffs[2] * diffs[2]) * (row[3] * row[3])
        ratio = square * lax.rsqrt(jnp.maximum(square, 1e-30))
        return diffs, jnp.maximum(1.0 - ratio, 0.0)

    def task(t):
        recv, k = tasks_ref[0, t], tasks_ref[1, t]
        rows = receiver(groups + recv // cells, lax.rem(recv, cells))
        return rows, jnp.transpose(pool[k // cells, lax.rem(k, cells)])

    def density(t, carry):
        rows, source = task(t)
        total = [jnp.zeros((CHUNK, LANES), jnp.float32) for _ in range(HALVES)]
        for s, q, col in chunks(source):
            for h in range(HALVES):
                _, u = inside(rows[h], col)
                u2 = u * u
                total[h] = total[h] + (u2 * u2) * (5.0 - 4.0 * u) * col[3]
        for h in range(HALVES):
            value = jnp.sum(total[h], axis=0, keepdims=True)
            inv = rows[h][3]
            parts[own, pl.ds(t * HALVES + h, 1), :] = value * (inv * inv * inv) * DENSITY_SCALE
        return carry

    lax.fori_loop(0, pairs, density, 0)
    second = [exchange(parts, psend_sem, precv_sem, e, g, n) for n, (e, g) in enumerate(peers)]
    for copy in second:
        copy.start()

    def prepare(t, carry):
        rows, source = task(t)
        total = [[jnp.zeros((CHUNK, LANES), jnp.float32) for _ in range(3)] for _ in range(HALVES)]
        for s, q, col in chunks(source):
            for h in range(HALVES):
                diffs, u = inside(rows[h], col)
                coeff = (u * u) * u * col[3]
                for d in range(3):
                    term = coeff * diffs[d]
                    waiting[t, d * HALVES + h, pl.ds(s * LANES + q, CHUNK), :] = term
                    total[h][d] = total[h][d] + term
        for h in range(HALVES):
            inv = rows[h][3]
            early[t, pl.ds(3 * HALVES + h, 1), :] = FORCE_SCALE * (inv * inv) * (inv * inv) * inv
            for d in range(3):
                early[t, pl.ds(d * HALVES + h, 1), :] = jnp.sum(total[h][d], axis=0, keepdims=True)
        return carry

    lax.fori_loop(0, pairs, prepare, 0)

    for e, g in far:
        tail_copy(e, g, 0, lax.rem(member + g, groups)).wait_recv()
    for slot in range(3 * groups):
        for c in range(cells):
            m = pool[slot, c, pl.ds(3 * HALVES, HALVES), :]
            inv = 1.0 / tail_of(slot)[pl.ds(c * HALVES, HALVES), :]
            rho[pl.ds((slot * cells + c) * HALVES, HALVES), :] = m * (inv * inv * inv) * DENSITY_SCALE

    for e, g in peers:
        arrival(parts, psend_sem, precv_sem, e, g).wait_recv()

    span = slab_cells * HALVES
    index = lax.broadcasted_iota(jnp.int32, (span, LANES), 0)
    odd = lax.rem(index, HALVES)
    cell_of = (index // HALVES).astype(jnp.float32)
    for d in range(3):
        total = rho[pl.ds(d * span, span), :]
        for g in range(groups):
            slot = d * groups + g
            part = parts[slot]
            to = tail_of(slot)[...]
            for t in range(pairs):
                value = part[t * HALVES:t * HALVES + 1]
                for h in range(1, HALVES):
                    value = jnp.where(odd == h, part[t * HALVES + h:t * HALVES + h + 1], value)
                at = to[cells * HALVES + t:cells * HALVES + t + 1]
                total = total + jnp.where(cell_of == at, value, 0.0)
        rho[pl.ds(d * span, span), :] = total

    source_rho = [rho[pl.ds(tasks_ref[1, t] * HALVES, HALVES), :] for t in range(pairs)]
    source_rho = 1.0 / jnp.maximum(jnp.concatenate(source_rho, axis=0), 1e-30)
    columns = jnp.transpose(source_rho)
    to_cell = [None] * slab_cells
    for t in range(pairs):
        recv = tasks_ref[0, t]
        a_rho = 1.0 / jnp.maximum(rho[pl.ds((slab_cells + recv) * HALVES, HALVES), :], 1e-30)
        total = [[jnp.zeros((CHUNK, LANES), jnp.float32) for _ in range(3)] for _ in range(HALVES)]
        for s in range(HALVES):
            for q in range(0, LANES, CHUNK):
                col = columns[q:q + CHUNK, t * HALVES + s:t * HALVES + s + 1]
                for h in range(HALVES):
                    for d in range(3):
                        term = waiting[t, d * HALVES + h, pl.ds(s * LANES + q, CHUNK), :]
                        total[h][d] = total[h][d] + term * col
        sums = []
        for d in range(3):
            for h in range(HALVES):
                at = pl.ds(d * HALVES + h, 1)
                value = jnp.sum(total[h][d], axis=0, keepdims=True) + early[t, at, :] * a_rho[h:h + 1]
                sums.append(value * early[t, pl.ds(3 * HALVES + h, 1), :])
        sums = jnp.concatenate(sums, axis=0)
        for cell in range(slab_cells):
            value = jnp.where(recv == cell, sums, 0.0)
            to_cell[cell] = value if t == 0 else to_cell[cell] + value

    rows = 3 * HALVES
    for cell in range(slab_cells):
        to_owner[cell // cells, pl.ds(cell % cells * rows, rows), :] = to_cell[cell]
    third = []
    for g in range(1, groups):
        copy = pltpu.make_async_remote_copy(
            src_ref=to_owner.at[lax.rem(member + g, groups)], dst_ref=forces.at[member], send_sem=fsend_sem.at[g],
            recv_sem=frecv_sem.at[member], device_id=place(0, g), device_id_type=MESH,
        )
        copy.start()
        third.append(copy)

    live = []
    for c in range(cells):
        for h in range(HALVES):
            live.append((lane + h * LANES < counts_ref[c]).astype(jnp.float32))
            at = pl.ds(c * HALVES + h, 1)
            rho_out[at, :] = rho[pl.ds((own * cells + c) * HALVES + h, 1), :] * live[-1]

    for copy in first + second:
        copy.wait_send()
    for g in range(1, groups):
        other = lax.rem(member + g, groups)
        pltpu.make_async_remote_copy(
            src_ref=to_owner.at[member], dst_ref=forces.at[other], send_sem=fsend_sem.at[0],
            recv_sem=frecv_sem.at[other], device_id=place(0, g), device_id_type=MESH,
        ).wait_recv()

    total = to_owner[member]
    for g in range(1, groups):
        total = total + forces[lax.rem(member + g, groups)]
    for c in range(cells):
        for h in range(HALVES):
            for d in range(3):
                at = (c * 3 + d) * HALVES + h
                acc_out[pl.ds(d, 1), pl.ds(c * CELL + h * LANES, LANES)] = total[at:at + 1] * live[c * HALVES + h]

    for copy in third:
        copy.wait_send()


def deliver(density_hbm, accel_hbm, density_out, accel_out, sems):
    copies = [
        pltpu.make_async_copy(density_hbm, density_out, sems.at[0]),
        pltpu.make_async_copy(accel_hbm, accel_out, sems.at[1]),
    ]
    for copy in copies:
        copy.start()
    for copy in copies:
        copy.wait()


def local(positions, mass, smooth, counts, tasks):
    groups, doms = lax.axis_size("grp"), lax.axis_size("dom")
    cells, pairs = counts.shape[0], tasks.shape[1]
    around = 3 * groups
    last = max(8, -(-(cells * HALVES + pairs) // 8) * 8)
    vmem, hbm = (pl.BlockSpec(memory_space=space) for space in (pltpu.VMEM, pltpu.HBM))
    density, accel = pl.pallas_call(
        functools.partial(kernel, doms, groups, cells, pairs),
        out_shape=(
            jax.ShapeDtypeStruct((cells * HALVES, LANES), jnp.float32),
            jax.ShapeDtypeStruct(positions.shape, jnp.float32),
        ),
        in_specs=[hbm] * 5,
        out_specs=(vmem, vmem),
        scratch_shapes=[
            pltpu.SMEM(tasks.shape, jnp.int32),
            pltpu.SMEM(counts.shape, jnp.int32),
            pltpu.VMEM(positions.shape, jnp.float32),
            pltpu.VMEM((1, mass.shape[0]), jnp.float32),
            pltpu.VMEM((1, smooth.shape[0]), jnp.float32),
            pltpu.VMEM((around, cells, 4 * HALVES, LANES), jnp.float32),
            pltpu.VMEM((groups, last, LANES), jnp.float32),
            pltpu.VMEM((around, last, LANES), jnp.float32),
            pltpu.VMEM((around, pairs * HALVES, LANES), jnp.float32),
            pltpu.VMEM((around * cells * HALVES, LANES), jnp.float32),
            pltpu.VMEM((groups, cells * 3 * HALVES, LANES), jnp.float32),
            pltpu.VMEM((groups, cells * 3 * HALVES, LANES), jnp.float32),
            pltpu.VMEM((pairs, 3 * HALVES, CELL, LANES), jnp.float32),
            pltpu.VMEM((pairs, 4 * HALVES, LANES), jnp.float32),
            pltpu.SemaphoreType.DMA((5,)),
            pltpu.SemaphoreType.DMA((around,)),
            pltpu.SemaphoreType.DMA((around,)),
            pltpu.SemaphoreType.DMA((around,)),
            pltpu.SemaphoreType.DMA((around,)),
            pltpu.SemaphoreType.DMA((around,)),
            pltpu.SemaphoreType.DMA((around,)),
            pltpu.SemaphoreType.DMA((groups,)),
            pltpu.SemaphoreType.DMA((groups,)),
        ],
        compiler_params=pltpu.CompilerParams(
            collective_id=0, has_side_effects=True, vmem_limit_bytes=64 * 1024 * 1024
        ),
    )(tasks, counts, positions, mass[None], smooth[None])
    return pl.pallas_call(
        deliver,
        out_shape=(
            jax.ShapeDtypeStruct(mass.shape, jnp.float32),
            jax.ShapeDtypeStruct(positions.shape, jnp.float32),
        ),
        in_specs=[hbm] * 2,
        out_specs=(hbm, hbm),
        scratch_shapes=[pltpu.SemaphoreType.DMA((2,))],
        compiler_params=pltpu.CompilerParams(vmem_limit_bytes=64 * 1024 * 1024),
    )(density.reshape(-1), accel)


def solution(mesh):
    in_specs = (
        P(None, ("dom", "grp")),
        P(("dom", "grp")),
        P(("dom", "grp")),
        P(("dom", "grp")),
        P(None, ("dom", "grp")),
    )
    out_specs = (P(("dom", "grp")), P(None, ("dom", "grp")))
    return jax.shard_map(local, mesh=mesh, in_specs=in_specs, out_specs=out_specs, check_vma=False)
```

```python
import functools
import math

import jax
import jax.numpy as jnp
from jax import lax
from jax.experimental import pallas as pl
from jax.experimental.pallas import tpu as pltpu
from jax.sharding import PartitionSpec as P

CELL = 256
LANES = 128
HALVES = CELL // LANES
CHUNK = 32
MESH = pl.DeviceIdType.MESH
DENSITY_SCALE = 21.0 / (2.0 * math.pi)
FORCE_SCALE = 105.0 / math.pi


def kernel(
    doms, groups, cells, pairs, tasks_hbm, counts_hbm, pos_hbm, mass_hbm, smooth_hbm,
    rho_out, acc_out,
    tasks_ref, counts_ref, pos_ref, mass_ref, smooth_ref,
    pool, tail, slab_tail, parts, rho, to_owner, forces, waiting, early,
    in_sem, main_sem, near_sem, far_sem, parts_sem, force_sem,
):
    slab_cells = groups * cells
    dom = lax.axis_index("dom")
    member = lax.axis_index("grp")
    own = groups + member
    around = 3 * groups

    def place(e, z):
        return (lax.rem(dom + e + doms, doms), z)

    def each_far(act):
        def step(i, carry):
            act(2 * lax.div(i, groups) - 1, lax.rem(member + i, groups), i)
            return carry

        lax.fori_loop(0, 2 * groups, step, 0)

    def each_near(act):
        def step(g, carry):
            act(0, lax.rem(member + g, groups), 2 * groups + g)
            return carry

        lax.fori_loop(1, groups, step, 0)

    def each(act):
        each_far(act)
        each_near(act)

    def start(ref, sems):
        def copy(e, z, n):
            slot = (1 - e) * groups + member
            pltpu.make_async_remote_copy(
                src_ref=ref.at[own], dst_ref=ref.at[slot], send_sem=sems.at[0], recv_sem=sems.at[1],
                device_id=place(e, z), device_id_type=MESH,
            ).start()

        return copy

    def whole(ref, sems, count):
        return pltpu.make_async_remote_copy(
            src_ref=ref.at[pl.ds(0, count)], dst_ref=ref.at[pl.ds(0, count)], send_sem=sems.at[0],
            recv_sem=sems.at[1], device_id=place(0, lax.rem(member + 1, groups)), device_id_type=MESH,
        )

    barrier = pltpu.get_barrier_semaphore()
    each(lambda e, z, n: pl.semaphore_signal(barrier, inc=1, device_id=place(e, z), device_id_type=MESH))
    moves = (
        (tasks_hbm, tasks_ref), (counts_hbm, counts_ref), (pos_hbm, pos_ref), (mass_hbm, mass_ref),
        (smooth_hbm, smooth_ref),
    )
    inputs = [pltpu.make_async_copy(*move, in_sem.at[n]) for n, move in enumerate(moves)]
    for copy in inputs:
        copy.start()
    for copy in inputs:
        copy.wait()

    lane = lax.broadcasted_iota(jnp.int32, (1, LANES), 1)
    for c in range(cells):
        for h in range(HALVES):
            at = pl.ds(c * CELL + h * LANES, LANES)
            live = (lane + h * LANES < counts_ref[c]).astype(jnp.float32)
            for d in range(3):
                pool[own, c, pl.ds(d * HALVES + h, 1), :] = pos_ref[pl.ds(d, 1), at]
            pool[own, c, pl.ds(3 * HALVES + h, 1), :] = mass_ref[:, at] * live
            tail[own, pl.ds(c * HALVES + h, 1), :] = smooth_ref[:, at]
    for t in range(pairs):
        tail[own, pl.ds(cells * HALVES + t, 1), :] = jnp.full((1, LANES), tasks_ref[0, t]).astype(jnp.float32)

    pl.semaphore_wait(barrier, around - 1)
    each(start(pool, main_sem))
    each_near(start(tail, near_sem))
    each_far(start(tail, far_sem))
    whole(pool, main_sem, around - 1).wait_recv()
    whole(tail, near_sem, groups - 1).wait_recv()
    slab_tail[...] = tail[pl.ds(groups, groups)]

    def receiver(slot, cell):
        block = pool[slot, cell]
        lengths = slab_tail[slot - groups]
        length = lengths[0:HALVES]
        for c in range(1, cells):
            length = jnp.where(cell == c, lengths[c * HALVES:(c + 1) * HALVES], length)
        inverse = 1.0 / length
        rows = []
        for h in range(HALVES):
            rows.append([block[d * HALVES + h:d * HALVES + h + 1] for d in range(3)] + [inverse[h:h + 1]])
        return rows

    def chunks(source):
        for s in range(HALVES):
            for q in range(0, LANES, CHUNK):
                yield s, q, [source[q:q + CHUNK, d * HALVES + s:d * HALVES + s + 1] for d in range(4)]

    def inside(row, col):
        diffs = [row[d] - col[d] for d in range(3)]
        square = (diffs[0] * diffs[0] + diffs[1] * diffs[1] + diffs[2] * diffs[2]) * (row[3] * row[3])
        ratio = square * lax.rsqrt(jnp.maximum(square, 1e-30))
        return diffs, jnp.maximum(1.0 - ratio, 0.0)

    def task(t):
        recv, k = tasks_ref[0, t], tasks_ref[1, t]
        rows = receiver(groups + recv // cells, lax.rem(recv, cells))
        return rows, jnp.transpose(pool[k // cells, lax.rem(k, cells)])

    def density(t, carry):
        rows, source = task(t)
        total = [jnp.zeros((CHUNK, LANES), jnp.float32) for _ in range(HALVES)]
        for s, q, col in chunks(source):
            for h in range(HALVES):
                _, u = inside(rows[h], col)
                u2 = u * u
                total[h] = total[h] + (u2 * u2) * (5.0 - 4.0 * u) * col[3]
        for h in range(HALVES):
            value = jnp.sum(total[h], axis=0, keepdims=True)
            inv = rows[h][3]
            parts[own, pl.ds(t * HALVES + h, 1), :] = value * (inv * inv * inv) * DENSITY_SCALE
        return carry

    lax.fori_loop(0, pairs, density, 0)
    each(start(parts, parts_sem))

    def prepare(t, carry):
        rows, source = task(t)
        total = [[jnp.zeros((CHUNK, LANES), jnp.float32) for _ in range(3)] for _ in range(HALVES)]
        for s, q, col in chunks(source):
            for h in range(HALVES):
                diffs, u = inside(rows[h], col)
                coeff = (u * u) * u * col[3]
                for d in range(3):
                    term = coeff * diffs[d]
                    waiting[t, d * HALVES + h, pl.ds(s * LANES + q, CHUNK), :] = term
                    total[h][d] = total[h][d] + term
        for h in range(HALVES):
            inv = rows[h][3]
            early[t, pl.ds(3 * HALVES + h, 1), :] = FORCE_SCALE * (inv * inv) * (inv * inv) * inv
            for d in range(3):
                early[t, pl.ds(d * HALVES + h, 1), :] = jnp.sum(total[h][d], axis=0, keepdims=True)
        return carry

    lax.fori_loop(0, pairs, prepare, 0)

    whole(tail, far_sem, 2 * groups).wait_recv()
    for slot in range(3 * groups):
        for c in range(cells):
            m = pool[slot, c, pl.ds(3 * HALVES, HALVES), :]
            inv = 1.0 / tail[slot, pl.ds(c * HALVES, HALVES), :]
            rho[pl.ds((slot * cells + c) * HALVES, HALVES), :] = m * (inv * inv * inv) * DENSITY_SCALE

    whole(parts, parts_sem, around - 1).wait_recv()

    span = slab_cells * HALVES
    index = lax.broadcasted_iota(jnp.int32, (span, LANES), 0)
    odd = lax.rem(index, HALVES)
    cell_of = (index // HALVES).astype(jnp.float32)
    for d in range(3):
        total = rho[pl.ds(d * span, span), :]
        for g in range(groups):
            slot = d * groups + g
            part = parts[slot]
            to = tail[slot]
            for t in range(pairs):
                value = part[t * HALVES:t * HALVES + 1]
                for h in range(1, HALVES):
                    value = jnp.where(odd == h, part[t * HALVES + h:t * HALVES + h + 1], value)
                at = to[cells * HALVES + t:cells * HALVES + t + 1]
                total = total + jnp.where(cell_of == at, value, 0.0)
        rho[pl.ds(d * span, span), :] = total

    source_rho = [rho[pl.ds(tasks_ref[1, t] * HALVES, HALVES), :] for t in range(pairs)]
    source_rho = 1.0 / jnp.maximum(jnp.concatenate(source_rho, axis=0), 1e-30)
    columns = jnp.transpose(source_rho)
    to_cell = [None] * slab_cells
    for t in range(pairs):
        recv = tasks_ref[0, t]
        a_rho = 1.0 / jnp.maximum(rho[pl.ds((slab_cells + recv) * HALVES, HALVES), :], 1e-30)
        total = [[jnp.zeros((CHUNK, LANES), jnp.float32) for _ in range(3)] for _ in range(HALVES)]
        for s in range(HALVES):
            for q in range(0, LANES, CHUNK):
                col = columns[q:q + CHUNK, t * HALVES + s:t * HALVES + s + 1]
                for h in range(HALVES):
                    for d in range(3):
                        term = waiting[t, d * HALVES + h, pl.ds(s * LANES + q, CHUNK), :]
                        total[h][d] = total[h][d] + term * col
        sums = []
        for d in range(3):
            for h in range(HALVES):
                at = pl.ds(d * HALVES + h, 1)
                value = jnp.sum(total[h][d], axis=0, keepdims=True) + early[t, at, :] * a_rho[h:h + 1]
                sums.append(value * early[t, pl.ds(3 * HALVES + h, 1), :])
        sums = jnp.concatenate(sums, axis=0)
        for cell in range(slab_cells):
            value = jnp.where(recv == cell, sums, 0.0)
            to_cell[cell] = value if t == 0 else to_cell[cell] + value

    rows = 3 * HALVES
    for cell in range(slab_cells):
        to_owner[cell // cells, pl.ds(cell % cells * rows, rows), :] = to_cell[cell]

    def owner_copy(e, z, n):
        pltpu.make_async_remote_copy(
            src_ref=to_owner.at[z], dst_ref=forces.at[member], send_sem=force_sem.at[0], recv_sem=force_sem.at[1],
            device_id=place(0, z), device_id_type=MESH,
        ).start()

    each_near(owner_copy)

    live = []
    for c in range(cells):
        for h in range(HALVES):
            live.append((lane + h * LANES < counts_ref[c]).astype(jnp.float32))
            at = pl.ds(c * HALVES + h, 1)
            rho_out[at, :] = rho[pl.ds((own * cells + c) * HALVES + h, 1), :] * live[-1]

    whole(pool, main_sem, around - 1).wait_send()
    whole(tail, near_sem, groups - 1).wait_send()
    whole(tail, far_sem, 2 * groups).wait_send()
    whole(parts, parts_sem, around - 1).wait_send()
    whole(forces, force_sem, groups - 1).wait_recv()

    total = to_owner[member]
    for g in range(1, groups):
        total = total + forces[lax.rem(member + g, groups)]
    for c in range(cells):
        for h in range(HALVES):
            for d in range(3):
                at = (c * 3 + d) * HALVES + h
                acc_out[pl.ds(d, 1), pl.ds(c * CELL + h * LANES, LANES)] = total[at:at + 1] * live[c * HALVES + h]

    whole(forces, force_sem, groups - 1).wait_send()


def deliver(density_hbm, accel_hbm, density_out, accel_out, sems):
    copies = [
        pltpu.make_async_copy(density_hbm, density_out, sems.at[0]),
        pltpu.make_async_copy(accel_hbm, accel_out, sems.at[1]),
    ]
    for copy in copies:
        copy.start()
    for copy in copies:
        copy.wait()


def local(positions, mass, smooth, counts, tasks):
    groups, doms = lax.axis_size("grp"), lax.axis_size("dom")
    cells, pairs = counts.shape[0], tasks.shape[1]
    around = 3 * groups
    last = max(8, -(-(cells * HALVES + pairs) // 8) * 8)
    vmem, hbm = (pl.BlockSpec(memory_space=space) for space in (pltpu.VMEM, pltpu.HBM))
    density, accel = pl.pallas_call(
        functools.partial(kernel, doms, groups, cells, pairs),
        out_shape=(
            jax.ShapeDtypeStruct((cells * HALVES, LANES), jnp.float32),
            jax.ShapeDtypeStruct(positions.shape, jnp.float32),
        ),
        in_specs=[hbm] * 5,
        out_specs=(vmem, vmem),
        scratch_shapes=[
            pltpu.SMEM(tasks.shape, jnp.int32),
            pltpu.SMEM(counts.shape, jnp.int32),
            pltpu.VMEM(positions.shape, jnp.float32),
            pltpu.VMEM((1, mass.shape[0]), jnp.float32),
            pltpu.VMEM((1, smooth.shape[0]), jnp.float32),
            pltpu.VMEM((around, cells, 4 * HALVES, LANES), jnp.float32),
            pltpu.VMEM((around, last, LANES), jnp.float32),
            pltpu.VMEM((groups, last, LANES), jnp.float32),
            pltpu.VMEM((around, pairs * HALVES, LANES), jnp.float32),
            pltpu.VMEM((around * cells * HALVES, LANES), jnp.float32),
            pltpu.VMEM((groups, cells * 3 * HALVES, LANES), jnp.float32),
            pltpu.VMEM((groups, cells * 3 * HALVES, LANES), jnp.float32),
            pltpu.VMEM((pairs, 3 * HALVES, CELL, LANES), jnp.float32),
            pltpu.VMEM((pairs, 4 * HALVES, LANES), jnp.float32),
            pltpu.SemaphoreType.DMA((5,)),
            pltpu.SemaphoreType.DMA((2,)),
            pltpu.SemaphoreType.DMA((2,)),
            pltpu.SemaphoreType.DMA((2,)),
            pltpu.SemaphoreType.DMA((2,)),
            pltpu.SemaphoreType.DMA((2,)),
        ],
        compiler_params=pltpu.CompilerParams(
            collective_id=0, has_side_effects=True, vmem_limit_bytes=64 * 1024 * 1024
        ),
    )(tasks, counts, positions, mass[None], smooth[None])
    return pl.pallas_call(
        deliver,
        out_shape=(
            jax.ShapeDtypeStruct(mass.shape, jnp.float32),
            jax.ShapeDtypeStruct(positions.shape, jnp.float32),
        ),
        in_specs=[hbm] * 2,
        out_specs=(hbm, hbm),
        scratch_shapes=[pltpu.SemaphoreType.DMA((2,))],
        compiler_params=pltpu.CompilerParams(vmem_limit_bytes=64 * 1024 * 1024),
    )(density.reshape(-1), accel)


def solution(mesh):
    in_specs = (
        P(None, ("dom", "grp")),
        P(("dom", "grp")),
        P(("dom", "grp")),
        P(("dom", "grp")),
        P(None, ("dom", "grp")),
    )
    out_specs = (P(("dom", "grp")), P(None, ("dom", "grp")))
    return jax.shard_map(local, mesh=mesh, in_specs=in_specs, out_specs=out_specs, check_vma=False)
```

```python
import functools
import math

import jax
import jax.numpy as jnp
from jax import lax
from jax.experimental import pallas as pl
from jax.experimental.pallas import tpu as pltpu
from jax.sharding import PartitionSpec as P

CELL = 256
LANES = 128
HALVES = CELL // LANES
CHUNK = 32
MESH = pl.DeviceIdType.MESH
DENSITY_SCALE = 21.0 / (2.0 * math.pi)
FORCE_SCALE = 105.0 / math.pi


def kernel(
    doms, groups, cells, pairs, tasks_hbm, counts_hbm, pos_hbm, mass_hbm, smooth_hbm,
    rho_out, acc_out,
    tasks_ref, counts_ref, pos_ref, mass_ref, smooth_ref,
    pool, tail, slab_tail, parts, rho, to_owner, forces, waiting, early, columns, over_rho,
    in_sem, main_sem, near_sem, far_sem, parts_sem, force_sem,
):
    slab_cells = groups * cells
    dom = lax.axis_index("dom")
    member = lax.axis_index("grp")
    own = groups + member
    around = 3 * groups

    def place(e, z):
        return (lax.rem(dom + e + doms, doms), z)

    def each_far(act):
        def step(i, carry):
            act(2 * lax.div(i, groups) - 1, lax.rem(member + i, groups), i)
            return carry

        lax.fori_loop(0, 2 * groups, step, 0)

    def each_near(act):
        def step(g, carry):
            act(0, lax.rem(member + g, groups), 2 * groups + g)
            return carry

        lax.fori_loop(1, groups, step, 0)

    def each(act):
        each_far(act)
        each_near(act)

    def start(ref, sems):
        def copy(e, z, n):
            slot = (1 - e) * groups + member
            pltpu.make_async_remote_copy(
                src_ref=ref.at[own], dst_ref=ref.at[slot], send_sem=sems.at[0], recv_sem=sems.at[1],
                device_id=place(e, z), device_id_type=MESH,
            ).start()

        return copy

    def whole(ref, sems, count):
        return pltpu.make_async_remote_copy(
            src_ref=ref.at[pl.ds(0, count)], dst_ref=ref.at[pl.ds(0, count)], send_sem=sems.at[0],
            recv_sem=sems.at[1], device_id=place(0, lax.rem(member + 1, groups)), device_id_type=MESH,
        )

    barrier = pltpu.get_barrier_semaphore()
    each(lambda e, z, n: pl.semaphore_signal(barrier, inc=1, device_id=place(e, z), device_id_type=MESH))
    moves = (
        (tasks_hbm, tasks_ref), (counts_hbm, counts_ref), (pos_hbm, pos_ref), (mass_hbm, mass_ref),
        (smooth_hbm, smooth_ref),
    )
    inputs = [pltpu.make_async_copy(*move, in_sem.at[n]) for n, move in enumerate(moves)]
    for copy in inputs:
        copy.start()
    for copy in inputs:
        copy.wait()

    lane = lax.broadcasted_iota(jnp.int32, (1, LANES), 1)
    for c in range(cells):
        for h in range(HALVES):
            at = pl.ds(c * CELL + h * LANES, LANES)
            live = (lane + h * LANES < counts_ref[c]).astype(jnp.float32)
            for d in range(3):
                pool[own, c, pl.ds(d * HALVES + h, 1), :] = pos_ref[pl.ds(d, 1), at]
            pool[own, c, pl.ds(3 * HALVES + h, 1), :] = mass_ref[:, at] * live
            tail[own, pl.ds(c * HALVES + h, 1), :] = smooth_ref[:, at]
    for t in range(pairs):
        tail[own, pl.ds(cells * HALVES + t, 1), :] = jnp.full((1, LANES), tasks_ref[0, t]).astype(jnp.float32)

    pl.semaphore_wait(barrier, around - 1)
    each(start(pool, main_sem))
    each_near(start(tail, near_sem))
    each_far(start(tail, far_sem))
    whole(pool, main_sem, around - 1).wait_recv()
    whole(tail, near_sem, groups - 1).wait_recv()
    slab_tail[...] = tail[pl.ds(groups, groups)]

    def receiver(slot, cell):
        block = pool[slot, cell]
        lengths = slab_tail[slot - groups]
        length = lengths[0:HALVES]
        for c in range(1, cells):
            length = jnp.where(cell == c, lengths[c * HALVES:(c + 1) * HALVES], length)
        inverse = 1.0 / length
        rows = []
        for h in range(HALVES):
            rows.append([block[d * HALVES + h:d * HALVES + h + 1] for d in range(3)] + [inverse[h:h + 1]])
        return rows

    def chunks(step, init):
        def some(i, carry):
            block = columns[pl.ds(pl.multiple_of(i * CHUNK, CHUNK), CHUNK), :]
            for s in range(HALVES):
                carry = step(s, i, [block[:, d * HALVES + s:d * HALVES + s + 1] for d in range(4)], carry)
            return carry

        return lax.fori_loop(0, LANES // CHUNK, some, init)

    def inside(row, col):
        diffs = [row[d] - col[d] for d in range(3)]
        square = (diffs[0] * diffs[0] + diffs[1] * diffs[1] + diffs[2] * diffs[2]) * (row[3] * row[3])
        ratio = square * lax.rsqrt(jnp.maximum(square, 1e-30))
        return diffs, jnp.maximum(1.0 - ratio, 0.0)

    def task(t):
        recv, k = tasks_ref[0, t], tasks_ref[1, t]
        rows = receiver(groups + recv // cells, lax.rem(recv, cells))
        columns[...] = jnp.transpose(pool[k // cells, lax.rem(k, cells)])
        return rows

    def density(t, carry):
        rows = task(t)

        def step(s, i, col, total):
            new = []
            for h in range(HALVES):
                _, u = inside(rows[h], col)
                u2 = u * u
                new.append(total[h] + (u2 * u2) * (5.0 - 4.0 * u) * col[3])
            return tuple(new)

        total = chunks(step, tuple(jnp.zeros((CHUNK, LANES), jnp.float32) for _ in range(HALVES)))
        for h in range(HALVES):
            value = jnp.sum(total[h], axis=0, keepdims=True)
            inv = rows[h][3]
            parts[own, pl.ds(t * HALVES + h, 1), :] = value * (inv * inv * inv) * DENSITY_SCALE
        return carry

    lax.fori_loop(0, pairs, density, 0)
    each(start(parts, parts_sem))

    def prepare(t, carry):
        rows = task(t)

        def step(s, i, col, total):
            new = []
            for h in range(HALVES):
                diffs, u = inside(rows[h], col)
                coeff = (u * u) * u * col[3]
                for d in range(3):
                    term = coeff * diffs[d]
                    at = pl.ds(pl.multiple_of(s * LANES + i * CHUNK, CHUNK), CHUNK)
                    waiting[t, d * HALVES + h, at, :] = term
                    new.append(total[h * 3 + d] + term)
            return tuple(new)

        total = chunks(step, tuple(jnp.zeros((CHUNK, LANES), jnp.float32) for _ in range(3 * HALVES)))
        for h in range(HALVES):
            inv = rows[h][3]
            early[t, pl.ds(3 * HALVES + h, 1), :] = FORCE_SCALE * (inv * inv) * (inv * inv) * inv
            for d in range(3):
                early[t, pl.ds(d * HALVES + h, 1), :] = jnp.sum(total[h * 3 + d], axis=0, keepdims=True)
        return carry

    lax.fori_loop(0, pairs, prepare, 0)

    whole(tail, far_sem, 2 * groups).wait_recv()
    for slot in range(3 * groups):
        for c in range(cells):
            m = pool[slot, c, pl.ds(3 * HALVES, HALVES), :]
            inv = 1.0 / tail[slot, pl.ds(c * HALVES, HALVES), :]
            rho[pl.ds((slot * cells + c) * HALVES, HALVES), :] = m * (inv * inv * inv) * DENSITY_SCALE

    whole(parts, parts_sem, around - 1).wait_recv()

    span = slab_cells * HALVES
    index = lax.broadcasted_iota(jnp.int32, (span, LANES), 0)
    odd = lax.rem(index, HALVES)
    cell_of = (index // HALVES).astype(jnp.float32)
    for d in range(3):
        total = rho[pl.ds(d * span, span), :]
        for g in range(groups):
            slot = d * groups + g
            part = parts[slot]
            to = tail[slot]
            for t in range(pairs):
                value = part[t * HALVES:t * HALVES + 1]
                for h in range(1, HALVES):
                    value = jnp.where(odd == h, part[t * HALVES + h:t * HALVES + h + 1], value)
                at = to[cells * HALVES + t:cells * HALVES + t + 1]
                total = total + jnp.where(cell_of == at, value, 0.0)
        rho[pl.ds(d * span, span), :] = total

    for t in range(pairs):
        k_rho = 1.0 / jnp.maximum(rho[pl.ds(tasks_ref[1, t] * HALVES, HALVES), :], 1e-30)
        over_rho[t] = jnp.transpose(jnp.concatenate([k_rho] * (8 // HALVES), axis=0))
    to_owner[...] = jnp.zeros_like(to_owner)
    rows = 3 * HALVES

    def finish(t, carry):
        recv = tasks_ref[0, t]
        a_rho = 1.0 / jnp.maximum(rho[pl.ds((slab_cells + recv) * HALVES, HALVES), :], 1e-30)
        total = [[jnp.zeros((CHUNK, LANES), jnp.float32) for _ in range(3)] for _ in range(HALVES)]
        for s in range(HALVES):
            for q in range(0, LANES, CHUNK):
                col = over_rho[t, pl.ds(q, CHUNK), pl.ds(s, 1)]
                for h in range(HALVES):
                    for d in range(3):
                        term = waiting[t, d * HALVES + h, pl.ds(s * LANES + q, CHUNK), :]
                        total[h][d] = total[h][d] + term * col
        sums = []
        for d in range(3):
            for h in range(HALVES):
                at = pl.ds(d * HALVES + h, 1)
                value = jnp.sum(total[h][d], axis=0, keepdims=True) + early[t, at, :] * a_rho[h:h + 1]
                sums.append(value * early[t, pl.ds(3 * HALVES + h, 1), :])
        sums = jnp.concatenate(sums, axis=0)
        for cell in range(slab_cells):
            at = pl.ds(cell % cells * rows, rows)
            to_owner[cell // cells, at, :] += jnp.where(recv == cell, sums, 0.0)
        return carry

    lax.fori_loop(0, pairs, finish, 0)

    def owner_copy(e, z, n):
        pltpu.make_async_remote_copy(
            src_ref=to_owner.at[z], dst_ref=forces.at[member], send_sem=force_sem.at[0], recv_sem=force_sem.at[1],
            device_id=place(0, z), device_id_type=MESH,
        ).start()

    each_near(owner_copy)

    live = []
    for c in range(cells):
        for h in range(HALVES):
            live.append((lane + h * LANES < counts_ref[c]).astype(jnp.float32))
            at = pl.ds(c * HALVES + h, 1)
            rho_out[at, :] = rho[pl.ds((own * cells + c) * HALVES + h, 1), :] * live[-1]

    whole(pool, main_sem, around - 1).wait_send()
    whole(tail, near_sem, groups - 1).wait_send()
    whole(tail, far_sem, 2 * groups).wait_send()
    whole(parts, parts_sem, around - 1).wait_send()
    whole(forces, force_sem, groups - 1).wait_recv()

    total = to_owner[member]
    for g in range(1, groups):
        total = total + forces[lax.rem(member + g, groups)]
    for c in range(cells):
        for h in range(HALVES):
            for d in range(3):
                at = (c * 3 + d) * HALVES + h
                acc_out[pl.ds(d, 1), pl.ds(c * CELL + h * LANES, LANES)] = total[at:at + 1] * live[c * HALVES + h]

    whole(forces, force_sem, groups - 1).wait_send()


def deliver(density_hbm, accel_hbm, density_out, accel_out, sems):
    copies = [
        pltpu.make_async_copy(density_hbm, density_out, sems.at[0]),
        pltpu.make_async_copy(accel_hbm, accel_out, sems.at[1]),
    ]
    for copy in copies:
        copy.start()
    for copy in copies:
        copy.wait()


def local(positions, mass, smooth, counts, tasks):
    groups, doms = lax.axis_size("grp"), lax.axis_size("dom")
    cells, pairs = counts.shape[0], tasks.shape[1]
    around = 3 * groups
    last = max(8, -(-(cells * HALVES + pairs) // 8) * 8)
    vmem, hbm = (pl.BlockSpec(memory_space=space) for space in (pltpu.VMEM, pltpu.HBM))
    density, accel = pl.pallas_call(
        functools.partial(kernel, doms, groups, cells, pairs),
        out_shape=(
            jax.ShapeDtypeStruct((cells * HALVES, LANES), jnp.float32),
            jax.ShapeDtypeStruct(positions.shape, jnp.float32),
        ),
        in_specs=[hbm] * 5,
        out_specs=(vmem, vmem),
        scratch_shapes=[
            pltpu.SMEM(tasks.shape, jnp.int32),
            pltpu.SMEM(counts.shape, jnp.int32),
            pltpu.VMEM(positions.shape, jnp.float32),
            pltpu.VMEM((1, mass.shape[0]), jnp.float32),
            pltpu.VMEM((1, smooth.shape[0]), jnp.float32),
            pltpu.VMEM((around, cells, 4 * HALVES, LANES), jnp.float32),
            pltpu.VMEM((around, last, LANES), jnp.float32),
            pltpu.VMEM((groups, last, LANES), jnp.float32),
            pltpu.VMEM((around, pairs * HALVES, LANES), jnp.float32),
            pltpu.VMEM((around * cells * HALVES, LANES), jnp.float32),
            pltpu.VMEM((groups, cells * 3 * HALVES, LANES), jnp.float32),
            pltpu.VMEM((groups, cells * 3 * HALVES, LANES), jnp.float32),
            pltpu.VMEM((pairs, 3 * HALVES, CELL, LANES), jnp.float32),
            pltpu.VMEM((pairs, 4 * HALVES, LANES), jnp.float32),
            pltpu.VMEM((LANES, 4 * HALVES), jnp.float32),
            pltpu.VMEM((pairs, LANES, 8), jnp.float32),
            pltpu.SemaphoreType.DMA((5,)),
            pltpu.SemaphoreType.DMA((2,)),
            pltpu.SemaphoreType.DMA((2,)),
            pltpu.SemaphoreType.DMA((2,)),
            pltpu.SemaphoreType.DMA((2,)),
            pltpu.SemaphoreType.DMA((2,)),
        ],
        compiler_params=pltpu.CompilerParams(
            collective_id=0, has_side_effects=True, vmem_limit_bytes=64 * 1024 * 1024
        ),
    )(tasks, counts, positions, mass[None], smooth[None])
    return pl.pallas_call(
        deliver,
        out_shape=(
            jax.ShapeDtypeStruct(mass.shape, jnp.float32),
            jax.ShapeDtypeStruct(positions.shape, jnp.float32),
        ),
        in_specs=[hbm] * 2,
        out_specs=(hbm, hbm),
        scratch_shapes=[pltpu.SemaphoreType.DMA((2,))],
        compiler_params=pltpu.CompilerParams(vmem_limit_bytes=64 * 1024 * 1024),
    )(density.reshape(-1), accel)


def solution(mesh):
    in_specs = (
        P(None, ("dom", "grp")),
        P(("dom", "grp")),
        P(("dom", "grp")),
        P(("dom", "grp")),
        P(None, ("dom", "grp")),
    )
    out_specs = (P(("dom", "grp")), P(None, ("dom", "grp")))
    return jax.shard_map(local, mesh=mesh, in_specs=in_specs, out_specs=out_specs, check_vma=False)
```

```python
import functools
import math

import jax
import jax.numpy as jnp
from jax import lax
from jax.experimental import pallas as pl
from jax.experimental.pallas import tpu as pltpu
from jax.sharding import PartitionSpec as P

CELL = 256
LANES = 128
HALVES = CELL // LANES
CHUNK = 32
MESH = pl.DeviceIdType.MESH
DENSITY_SCALE = 21.0 / (2.0 * math.pi)
FORCE_SCALE = 105.0 / math.pi


def kernel(
    doms, groups, cells, pairs, tasks_hbm, counts_hbm, pos_hbm, mass_hbm, smooth_hbm,
    rho_out, forces,
    tasks_ref, counts_ref, pos_ref, mass_ref, smooth_ref,
    pool, tail, slab_tail, parts, rho, to_owner, rho_own, weights, waiting, early,
    in_sem, main_sem, near_sem, far_sem, parts_sem, force_sem,
):
    slab_cells = groups * cells
    dom = lax.axis_index("dom")
    member = lax.axis_index("grp")
    own = groups + member
    around = 3 * groups

    def place(e, z):
        return (lax.rem(dom + e + doms, doms), z)

    def each_far(act):
        def step(i, carry):
            act(2 * lax.div(i, groups) - 1, lax.rem(member + i, groups), i)
            return carry

        lax.fori_loop(0, 2 * groups, step, 0)

    def each_near(act):
        def step(g, carry):
            act(0, lax.rem(member + g, groups), 2 * groups + g)
            return carry

        lax.fori_loop(1, groups, step, 0)

    def each(act):
        each_far(act)
        each_near(act)

    def start(ref, sems):
        def copy(e, z, n):
            slot = (1 - e) * groups + member
            pltpu.make_async_remote_copy(
                src_ref=ref.at[own], dst_ref=ref.at[slot], send_sem=sems.at[0], recv_sem=sems.at[1],
                device_id=place(e, z), device_id_type=MESH,
            ).start()

        return copy

    def whole(ref, sems, count):
        return pltpu.make_async_remote_copy(
            src_ref=ref.at[pl.ds(0, count)], dst_ref=ref.at[pl.ds(0, count)], send_sem=sems.at[0],
            recv_sem=sems.at[1], device_id=place(0, lax.rem(member + 1, groups)), device_id_type=MESH,
        )

    barrier = pltpu.get_barrier_semaphore()
    each(lambda e, z, n: pl.semaphore_signal(barrier, inc=1, device_id=place(e, z), device_id_type=MESH))
    moves = (
        (tasks_hbm, tasks_ref), (counts_hbm, counts_ref), (pos_hbm, pos_ref), (mass_hbm, mass_ref),
        (smooth_hbm, smooth_ref),
    )
    inputs = [pltpu.make_async_copy(*move, in_sem.at[n]) for n, move in enumerate(moves)]
    for copy in inputs:
        copy.start()
    for copy in inputs:
        copy.wait()

    lane = lax.broadcasted_iota(jnp.int32, (1, LANES), 1)
    for c in range(cells):
        for h in range(HALVES):
            at = pl.ds(c * CELL + h * LANES, LANES)
            live = (lane + h * LANES < counts_ref[c]).astype(jnp.float32)
            for d in range(3):
                pool[own, c, pl.ds(d * HALVES + h, 1), :] = pos_ref[pl.ds(d, 1), at]
            pool[own, c, pl.ds(3 * HALVES + h, 1), :] = mass_ref[:, at] * live
            tail[own, pl.ds(c * HALVES + h, 1), :] = smooth_ref[:, at]
    for t in range(pairs):
        tail[own, pl.ds(cells * HALVES + t, 1), :] = jnp.full((1, LANES), tasks_ref[0, t]).astype(jnp.float32)

    pl.semaphore_wait(barrier, around - 1)
    each(start(pool, main_sem))
    each_near(start(tail, near_sem))
    each_far(start(tail, far_sem))
    whole(pool, main_sem, around - 1).wait_recv()
    whole(tail, near_sem, groups - 1).wait_recv()
    slab_tail[...] = tail[pl.ds(groups, groups)]

    def receiver(slot, cell):
        block = pool[slot, cell]
        lengths = slab_tail[slot - groups]
        length = lengths[0:HALVES]
        for c in range(1, cells):
            length = jnp.where(cell == c, lengths[c * HALVES:(c + 1) * HALVES], length)
        inverse = 1.0 / length
        rows = []
        for h in range(HALVES):
            rows.append([block[d * HALVES + h:d * HALVES + h + 1] for d in range(3)] + [inverse[h:h + 1], block[3 * HALVES + h:3 * HALVES + h + 1]])
        return rows

    def chunks(source):
        for s in range(HALVES):
            for q in range(0, LANES, CHUNK):
                yield s, q, [source[q:q + CHUNK, d * HALVES + s:d * HALVES + s + 1] for d in range(4)]

    def inside(row, col):
        diffs = [row[d] - col[d] for d in range(3)]
        square = (diffs[0] * diffs[0] + diffs[1] * diffs[1] + diffs[2] * diffs[2]) * (row[3] * row[3])
        ratio = square * lax.rsqrt(jnp.maximum(square, 1e-30))
        return jnp.maximum(1.0 - ratio, 0.0)

    def task(t):
        recv, k = tasks_ref[0, t], tasks_ref[1, t]
        rows = receiver(groups + recv // cells, lax.rem(recv, cells))
        return rows, jnp.transpose(pool[k // cells, lax.rem(k, cells)])

    for t in range(pairs):
        rows, source = task(t)
        total = [jnp.zeros((CHUNK, LANES), jnp.float32) for _ in range(HALVES)]
        for s, q, col in chunks(source):
            for h in range(HALVES):
                u = inside(rows[h], col)
                u2 = u * u
                heavy = u2 * col[3]
                weights[t, h, pl.ds(s * LANES + q, CHUNK), :] = heavy * u
                total[h] = total[h] + (heavy * u2) * (1.25 - u)
        for h in range(HALVES):
            value = jnp.sum(total[h], axis=0, keepdims=True)
            inv = rows[h][3]
            parts[own, pl.ds(t * HALVES + h, 1), :] = value * (inv * inv * inv) * (4.0 * DENSITY_SCALE)
    each(start(parts, parts_sem))

    def prepare(t, carry):
        rows, source = task(t)
        total = [[jnp.zeros((CHUNK, LANES), jnp.float32) for _ in range(3)] for _ in range(HALVES)]
        for s, q, col in chunks(source):
            for h in range(HALVES):
                weight = weights[t, h, pl.ds(s * LANES + q, CHUNK), :]
                for d in range(3):
                    term = weight * (rows[h][d] - col[d])
                    waiting[t, d * HALVES + h, pl.ds(s * LANES + q, CHUNK), :] = term
                    total[h][d] = total[h][d] + term
        for h in range(HALVES):
            inv = rows[h][3]
            fifth = FORCE_SCALE * (inv * inv) * (inv * inv) * inv
            early[t, pl.ds(3 * HALVES + h, 1), :] = jnp.where(rows[h][4] > 0.0, fifth, 0.0)
            for d in range(3):
                early[t, pl.ds(d * HALVES + h, 1), :] = jnp.sum(total[h][d], axis=0, keepdims=True)
        return carry

    lax.fori_loop(0, pairs, prepare, 0)

    whole(tail, far_sem, 2 * groups).wait_recv()
    for slot in range(3 * groups):
        for c in range(cells):
            m = pool[slot, c, pl.ds(3 * HALVES, HALVES), :]
            inv = 1.0 / tail[slot, pl.ds(c * HALVES, HALVES), :]
            rho[pl.ds((slot * cells + c) * HALVES, HALVES), :] = m * (inv * inv * inv) * DENSITY_SCALE

    whole(parts, parts_sem, around - 1).wait_recv()

    span = slab_cells * HALVES
    index = lax.broadcasted_iota(jnp.int32, (span, LANES), 0)
    odd = lax.rem(index, HALVES)
    cell_of = (index // HALVES).astype(jnp.float32)
    for d in range(3):
        total = rho[pl.ds(d * span, span), :]
        for g in range(groups):
            slot = d * groups + g
            part = parts[slot]
            to = tail[slot]
            for t in range(pairs):
                value = part[t * HALVES:t * HALVES + 1]
                for h in range(1, HALVES):
                    value = jnp.where(odd == h, part[t * HALVES + h:t * HALVES + h + 1], value)
                at = to[cells * HALVES + t:cells * HALVES + t + 1]
                total = total + jnp.where(cell_of == at, value, 0.0)
        rho[pl.ds(d * span, span), :] = total

    source_rho = [rho[pl.ds(tasks_ref[1, t] * HALVES, HALVES), :] for t in range(pairs)]
    source_rho = 1.0 / jnp.maximum(jnp.concatenate(source_rho, axis=0), 1e-30)
    columns = jnp.transpose(source_rho)
    to_cell = [None] * slab_cells
    for t in range(pairs):
        recv = tasks_ref[0, t]
        a_rho = 1.0 / jnp.maximum(rho[pl.ds((slab_cells + recv) * HALVES, HALVES), :], 1e-30)
        total = [[jnp.zeros((CHUNK, LANES), jnp.float32) for _ in range(3)] for _ in range(HALVES)]
        for s in range(HALVES):
            for q in range(0, LANES, CHUNK):
                col = columns[q:q + CHUNK, t * HALVES + s:t * HALVES + s + 1]
                for h in range(HALVES):
                    for d in range(3):
                        term = waiting[t, d * HALVES + h, pl.ds(s * LANES + q, CHUNK), :]
                        total[h][d] = total[h][d] + term * col
        sums = []
        for d in range(3):
            for h in range(HALVES):
                at = pl.ds(d * HALVES + h, 1)
                value = jnp.sum(total[h][d], axis=0, keepdims=True) + early[t, at, :] * a_rho[h:h + 1]
                sums.append(value * early[t, pl.ds(3 * HALVES + h, 1), :])
        sums = jnp.concatenate(sums, axis=0)
        for cell in range(slab_cells):
            value = jnp.where(recv == cell, sums, 0.0)
            to_cell[cell] = value if t == 0 else to_cell[cell] + value

    rows = 3 * HALVES
    for cell in range(slab_cells):
        to_owner[cell // cells, pl.ds(cell % cells * rows, rows), :] = to_cell[cell]

    def owner_copy(e, z, n):
        pltpu.make_async_remote_copy(
            src_ref=to_owner.at[z], dst_ref=forces.at[member], send_sem=force_sem.at[0], recv_sem=force_sem.at[1],
            device_id=place(0, z), device_id_type=MESH,
        ).start()

    each_near(owner_copy)

    for c in range(cells):
        for h in range(HALVES):
            live = (lane + h * LANES < counts_ref[c]).astype(jnp.float32)
            rho_own[pl.ds(c * HALVES + h, 1), :] = rho[pl.ds((own * cells + c) * HALVES + h, 1), :] * live
    outs = [
        pltpu.make_async_copy(to_owner.at[member], forces.at[member], in_sem.at[0]),
        pltpu.make_async_copy(rho_own, rho_out, in_sem.at[1]),
    ]
    for copy in outs:
        copy.start()

    whole(pool, main_sem, around - 1).wait_send()
    whole(tail, near_sem, groups - 1).wait_send()
    whole(tail, far_sem, 2 * groups).wait_send()
    whole(parts, parts_sem, around - 1).wait_send()
    for copy in outs:
        copy.wait()
    whole(forces, force_sem, groups - 1).wait_recv()
    whole(to_owner, force_sem, groups - 1).wait_send()


def deliver(density_hbm, forces_hbm, density_out, accel_out, density, forces, accel, sems):
    ins = [
        pltpu.make_async_copy(density_hbm, density, sems.at[0]),
        pltpu.make_async_copy(forces_hbm, forces, sems.at[1]),
    ]
    for copy in ins:
        copy.start()
    ins[0].wait()
    outs = [pltpu.make_async_copy(density, density_out, sems.at[2])]
    outs[0].start()
    ins[1].wait()
    total = forces[0]
    for g in range(1, forces.shape[0]):
        total = total + forces[g]
    for at in range(total.shape[0]):
        c, d, h = at // (3 * HALVES), at // HALVES % 3, at % HALVES
        accel[pl.ds(d, 1), pl.ds(c * CELL + h * LANES, LANES)] = total[at:at + 1]
    outs.append(pltpu.make_async_copy(accel, accel_out, sems.at[3]))
    outs[1].start()
    for copy in outs:
        copy.wait()


def local(positions, mass, smooth, counts, tasks):
    groups, doms = lax.axis_size("grp"), lax.axis_size("dom")
    cells, pairs = counts.shape[0], tasks.shape[1]
    around = 3 * groups
    last = max(8, -(-(cells * HALVES + pairs) // 8) * 8)
    hbm = pl.BlockSpec(memory_space=pltpu.HBM)
    density, forces = pl.pallas_call(
        functools.partial(kernel, doms, groups, cells, pairs),
        out_shape=(
            jax.ShapeDtypeStruct((cells * HALVES, LANES), jnp.float32),
            jax.ShapeDtypeStruct((groups, cells * 3 * HALVES, LANES), jnp.float32),
        ),
        in_specs=[hbm] * 5,
        out_specs=(hbm, hbm),
        scratch_shapes=[
            pltpu.SMEM(tasks.shape, jnp.int32),
            pltpu.SMEM(counts.shape, jnp.int32),
            pltpu.VMEM(positions.shape, jnp.float32),
            pltpu.VMEM((1, mass.shape[0]), jnp.float32),
            pltpu.VMEM((1, smooth.shape[0]), jnp.float32),
            pltpu.VMEM((around, cells, 4 * HALVES, LANES), jnp.float32),
            pltpu.VMEM((around, last, LANES), jnp.float32),
            pltpu.VMEM((groups, last, LANES), jnp.float32),
            pltpu.VMEM((around, pairs * HALVES, LANES), jnp.float32),
            pltpu.VMEM((around * cells * HALVES, LANES), jnp.float32),
            pltpu.VMEM((groups, cells * 3 * HALVES, LANES), jnp.float32),
            pltpu.VMEM((cells * HALVES, LANES), jnp.float32),
            pltpu.VMEM((pairs, HALVES, CELL, LANES), jnp.float32),
            pltpu.VMEM((pairs, 3 * HALVES, CELL, LANES), jnp.float32),
            pltpu.VMEM((pairs, 4 * HALVES, LANES), jnp.float32),
            pltpu.SemaphoreType.DMA((5,)),
            pltpu.SemaphoreType.DMA((2,)),
            pltpu.SemaphoreType.DMA((2,)),
            pltpu.SemaphoreType.DMA((2,)),
            pltpu.SemaphoreType.DMA((2,)),
            pltpu.SemaphoreType.DMA((2,)),
        ],
        compiler_params=pltpu.CompilerParams(
            collective_id=0, has_side_effects=True, vmem_limit_bytes=64 * 1024 * 1024
        ),
    )(tasks, counts, positions, mass[None], smooth[None])
    return pl.pallas_call(
        deliver,
        out_shape=(
            jax.ShapeDtypeStruct(mass.shape, jnp.float32),
            jax.ShapeDtypeStruct(positions.shape, jnp.float32),
        ),
        in_specs=[hbm] * 2,
        out_specs=(hbm, hbm),
        scratch_shapes=[
            pltpu.VMEM(mass.shape, jnp.float32),
            pltpu.VMEM(forces.shape, jnp.float32),
            pltpu.VMEM(positions.shape, jnp.float32),
            pltpu.SemaphoreType.DMA((4,)),
        ],
        compiler_params=pltpu.CompilerParams(vmem_limit_bytes=64 * 1024 * 1024),
    )(density.reshape(-1), forces)


def solution(mesh):
    in_specs = (
        P(None, ("dom", "grp")),
        P(("dom", "grp")),
        P(("dom", "grp")),
        P(("dom", "grp")),
        P(None, ("dom", "grp")),
    )
    out_specs = (P(("dom", "grp")), P(None, ("dom", "grp")))
    return jax.shard_map(local, mesh=mesh, in_specs=in_specs, out_specs=out_specs, check_vma=False)
```

```python
import functools
import math

import jax
import jax.numpy as jnp
from jax import lax
from jax.experimental import pallas as pl
from jax.experimental.pallas import tpu as pltpu
from jax.sharding import PartitionSpec as P

CELL = 256
LANES = 128
HALVES = CELL // LANES
CHUNK = 32
MESH = pl.DeviceIdType.MESH
DENSITY_SCALE = 21.0 / (2.0 * math.pi)
FORCE_SCALE = 105.0 / math.pi


def kernel(
    doms, groups, cells, pairs, tasks_hbm, counts_hbm, pos_hbm, mass_hbm, smooth_hbm,
    rho_out, forces,
    tasks_ref, counts_ref, pos_ref, mass_ref, smooth_ref,
    pool, tail, slab_tail, parts, rho, to_owner, rho_own, weights, waiting, early,
    in_sem, main_sem, near_sem, far_sem, parts_sem, force_sem,
):
    slab_cells = groups * cells
    dom = lax.axis_index("dom")
    member = lax.axis_index("grp")
    own = groups + member
    around = 3 * groups

    def place(e, z):
        return (lax.rem(dom + e + doms, doms), z)

    def each_far(act):
        def step(i, carry):
            act(2 * lax.div(i, groups) - 1, lax.rem(member + i, groups), i)
            return carry

        lax.fori_loop(0, 2 * groups, step, 0)

    def each_near(act):
        def step(g, carry):
            act(0, lax.rem(member + g, groups), 2 * groups + g)
            return carry

        lax.fori_loop(1, groups, step, 0)

    def each(act):
        each_far(act)
        each_near(act)

    def start(ref, sems):
        def copy(e, z, n):
            slot = (1 - e) * groups + member
            pltpu.make_async_remote_copy(
                src_ref=ref.at[own], dst_ref=ref.at[slot], send_sem=sems.at[0], recv_sem=sems.at[1],
                device_id=place(e, z), device_id_type=MESH,
            ).start()

        return copy

    def whole(ref, sems, count):
        return pltpu.make_async_remote_copy(
            src_ref=ref.at[pl.ds(0, count)], dst_ref=ref.at[pl.ds(0, count)], send_sem=sems.at[0],
            recv_sem=sems.at[1], device_id=place(0, lax.rem(member + 1, groups)), device_id_type=MESH,
        )

    barrier = pltpu.get_barrier_semaphore()
    each(lambda e, z, n: pl.semaphore_signal(barrier, inc=1, device_id=place(e, z), device_id_type=MESH))
    moves = (
        (tasks_hbm, tasks_ref), (counts_hbm, counts_ref), (pos_hbm, pos_ref), (mass_hbm, mass_ref),
        (smooth_hbm, smooth_ref),
    )
    inputs = [pltpu.make_async_copy(*move, in_sem.at[n]) for n, move in enumerate(moves)]
    for copy in inputs:
        copy.start()
    for copy in inputs:
        copy.wait()

    lane = lax.broadcasted_iota(jnp.int32, (1, LANES), 1)
    for c in range(cells):
        for h in range(HALVES):
            at = pl.ds(c * CELL + h * LANES, LANES)
            live = (lane + h * LANES < counts_ref[c]).astype(jnp.float32)
            for d in range(3):
                pool[own, c, pl.ds(d * HALVES + h, 1), :] = pos_ref[pl.ds(d, 1), at]
            pool[own, c, pl.ds(3 * HALVES + h, 1), :] = mass_ref[:, at] * live
            tail[own, pl.ds(c * HALVES + h, 1), :] = smooth_ref[:, at]
    for t in range(pairs):
        tail[own, pl.ds(cells * HALVES + t, 1), :] = jnp.full((1, LANES), tasks_ref[0, t]).astype(jnp.float32)

    pl.semaphore_wait(barrier, around - 1)
    each_near(start(tail, near_sem))
    each(start(pool, main_sem))
    whole(pool, main_sem, around - 1).wait_recv()
    whole(tail, near_sem, groups - 1).wait_recv()
    each_far(start(tail, far_sem))
    slab_tail[...] = tail[pl.ds(groups, groups)]

    def receiver(slot, cell):
        block = pool[slot, cell]
        lengths = slab_tail[slot - groups]
        length = lengths[0:HALVES]
        for c in range(1, cells):
            length = jnp.where(cell == c, lengths[c * HALVES:(c + 1) * HALVES], length)
        inverse = 1.0 / length
        rows = []
        for h in range(HALVES):
            rows.append([block[d * HALVES + h:d * HALVES + h + 1] for d in range(3)] + [inverse[h:h + 1], block[3 * HALVES + h:3 * HALVES + h + 1]])
        return rows

    def chunks(source):
        for s in range(HALVES):
            for q in range(0, LANES, CHUNK):
                yield s, q, [source[q:q + CHUNK, d * HALVES + s:d * HALVES + s + 1] for d in range(4)]

    def inside(row, col):
        diffs = [row[d] - col[d] for d in range(3)]
        square = (diffs[0] * diffs[0] + diffs[1] * diffs[1] + diffs[2] * diffs[2]) * (row[3] * row[3])
        ratio = square * lax.rsqrt(jnp.maximum(square, 1e-30))
        return jnp.maximum(1.0 - ratio, 0.0)

    def task(t):
        recv, k = tasks_ref[0, t], tasks_ref[1, t]
        rows = receiver(groups + recv // cells, lax.rem(recv, cells))
        return rows, jnp.transpose(pool[k // cells, lax.rem(k, cells)])

    for t in range(pairs):
        rows, source = task(t)
        total = [jnp.zeros((CHUNK, LANES), jnp.float32) for _ in range(HALVES)]
        for s, q, col in chunks(source):
            for h in range(HALVES):
                u = inside(rows[h], col)
                u2 = u * u
                heavy = u2 * col[3]
                weights[t, h, pl.ds(s * LANES + q, CHUNK), :] = heavy * u
                total[h] = total[h] + (heavy * u2) * (1.25 - u)
        for h in range(HALVES):
            value = jnp.sum(total[h], axis=0, keepdims=True)
            inv = rows[h][3]
            parts[own, pl.ds(t * HALVES + h, 1), :] = value * (inv * inv * inv) * (4.0 * DENSITY_SCALE)
    each(start(parts, parts_sem))

    def prepare(t, carry):
        rows, source = task(t)
        total = [[jnp.zeros((CHUNK, LANES), jnp.float32) for _ in range(3)] for _ in range(HALVES)]
        for s, q, col in chunks(source):
            for h in range(HALVES):
                weight = weights[t, h, pl.ds(s * LANES + q, CHUNK), :]
                for d in range(3):
                    term = weight * (rows[h][d] - col[d])
                    waiting[t, d * HALVES + h, pl.ds(s * LANES + q, CHUNK), :] = term
                    total[h][d] = total[h][d] + term
        for h in range(HALVES):
            inv = rows[h][3]
            fifth = FORCE_SCALE * (inv * inv) * (inv * inv) * inv
            early[t, pl.ds(3 * HALVES + h, 1), :] = jnp.where(rows[h][4] > 0.0, fifth, 0.0)
            for d in range(3):
                early[t, pl.ds(d * HALVES + h, 1), :] = jnp.sum(total[h][d], axis=0, keepdims=True)
        return carry

    lax.fori_loop(0, pairs, prepare, 0)

    whole(tail, far_sem, 2 * groups).wait_recv()
    for slot in range(3 * groups):
        for c in range(cells):
            m = pool[slot, c, pl.ds(3 * HALVES, HALVES), :]
            inv = 1.0 / tail[slot, pl.ds(c * HALVES, HALVES), :]
            rho[pl.ds((slot * cells + c) * HALVES, HALVES), :] = m * (inv * inv * inv) * DENSITY_SCALE

    whole(parts, parts_sem, around - 1).wait_recv()

    span = slab_cells * HALVES
    index = lax.broadcasted_iota(jnp.int32, (span, LANES), 0)
    odd = lax.rem(index, HALVES)
    cell_of = (index // HALVES).astype(jnp.float32)
    for d in range(3):
        total = rho[pl.ds(d * span, span), :]
        for g in range(groups):
            slot = d * groups + g
            part = parts[slot]
            to = tail[slot]
            for t in range(pairs):
                value = part[t * HALVES:t * HALVES + 1]
                for h in range(1, HALVES):
                    value = jnp.where(odd == h, part[t * HALVES + h:t * HALVES + h + 1], value)
                at = to[cells * HALVES + t:cells * HALVES + t + 1]
                total = total + jnp.where(cell_of == at, value, 0.0)
        rho[pl.ds(d * span, span), :] = total

    source_rho = [rho[pl.ds(tasks_ref[1, t] * HALVES, HALVES), :] for t in range(pairs)]
    source_rho = 1.0 / jnp.maximum(jnp.concatenate(source_rho, axis=0), 1e-30)
    columns = jnp.transpose(source_rho)
    to_cell = [None] * slab_cells
    for t in range(pairs):
        recv = tasks_ref[0, t]
        a_rho = 1.0 / jnp.maximum(rho[pl.ds((slab_cells + recv) * HALVES, HALVES), :], 1e-30)
        total = [[jnp.zeros((CHUNK, LANES), jnp.float32) for _ in range(3)] for _ in range(HALVES)]
        for s in range(HALVES):
            for q in range(0, LANES, CHUNK):
                col = columns[q:q + CHUNK, t * HALVES + s:t * HALVES + s + 1]
                for h in range(HALVES):
                    for d in range(3):
                        term = waiting[t, d * HALVES + h, pl.ds(s * LANES + q, CHUNK), :]
                        total[h][d] = total[h][d] + term * col
        sums = []
        for d in range(3):
            for h in range(HALVES):
                at = pl.ds(d * HALVES + h, 1)
                value = jnp.sum(total[h][d], axis=0, keepdims=True) + early[t, at, :] * a_rho[h:h + 1]
                sums.append(value * early[t, pl.ds(3 * HALVES + h, 1), :])
        sums = jnp.concatenate(sums, axis=0)
        for cell in range(slab_cells):
            value = jnp.where(recv == cell, sums, 0.0)
            to_cell[cell] = value if t == 0 else to_cell[cell] + value

    rows = 3 * HALVES
    for cell in range(slab_cells):
        to_owner[cell // cells, pl.ds(cell % cells * rows, rows), :] = to_cell[cell]

    def owner_copy(e, z, n):
        pltpu.make_async_remote_copy(
            src_ref=to_owner.at[z], dst_ref=forces.at[member], send_sem=force_sem.at[0], recv_sem=force_sem.at[1],
            device_id=place(0, z), device_id_type=MESH,
        ).start()

    each_near(owner_copy)

    for c in range(cells):
        for h in range(HALVES):
            live = (lane + h * LANES < counts_ref[c]).astype(jnp.float32)
            rho_own[pl.ds(c * HALVES + h, 1), :] = rho[pl.ds((own * cells + c) * HALVES + h, 1), :] * live
    outs = [
        pltpu.make_async_copy(to_owner.at[member], forces.at[member], in_sem.at[0]),
        pltpu.make_async_copy(rho_own, rho_out, in_sem.at[1]),
    ]
    for copy in outs:
        copy.start()

    whole(pool, main_sem, around - 1).wait_send()
    whole(tail, near_sem, groups - 1).wait_send()
    whole(tail, far_sem, 2 * groups).wait_send()
    whole(parts, parts_sem, around - 1).wait_send()
    for copy in outs:
        copy.wait()
    whole(forces, force_sem, groups - 1).wait_recv()
    whole(to_owner, force_sem, groups - 1).wait_send()


def deliver(density_hbm, forces_hbm, density_out, accel_out, density, forces, accel, sems):
    ins = [
        pltpu.make_async_copy(density_hbm, density, sems.at[0]),
        pltpu.make_async_copy(forces_hbm, forces, sems.at[1]),
    ]
    for copy in ins:
        copy.start()
    ins[0].wait()
    outs = [pltpu.make_async_copy(density, density_out, sems.at[2])]
    outs[0].start()
    ins[1].wait()
    total = forces[0]
    for g in range(1, forces.shape[0]):
        total = total + forces[g]
    for at in range(total.shape[0]):
        c, d, h = at // (3 * HALVES), at // HALVES % 3, at % HALVES
        accel[pl.ds(d, 1), pl.ds(c * CELL + h * LANES, LANES)] = total[at:at + 1]
    outs.append(pltpu.make_async_copy(accel, accel_out, sems.at[3]))
    outs[1].start()
    for copy in outs:
        copy.wait()


def local(positions, mass, smooth, counts, tasks):
    groups, doms = lax.axis_size("grp"), lax.axis_size("dom")
    cells, pairs = counts.shape[0], tasks.shape[1]
    around = 3 * groups
    last = max(8, -(-(cells * HALVES + pairs) // 8) * 8)
    hbm = pl.BlockSpec(memory_space=pltpu.HBM)
    density, forces = pl.pallas_call(
        functools.partial(kernel, doms, groups, cells, pairs),
        out_shape=(
            jax.ShapeDtypeStruct((cells * HALVES, LANES), jnp.float32),
            jax.ShapeDtypeStruct((groups, cells * 3 * HALVES, LANES), jnp.float32),
        ),
        in_specs=[hbm] * 5,
        out_specs=(hbm, hbm),
        scratch_shapes=[
            pltpu.SMEM(tasks.shape, jnp.int32),
            pltpu.SMEM(counts.shape, jnp.int32),
            pltpu.VMEM(positions.shape, jnp.float32),
            pltpu.VMEM((1, mass.shape[0]), jnp.float32),
            pltpu.VMEM((1, smooth.shape[0]), jnp.float32),
            pltpu.VMEM((around, cells, 4 * HALVES, LANES), jnp.float32),
            pltpu.VMEM((around, last, LANES), jnp.float32),
            pltpu.VMEM((groups, last, LANES), jnp.float32),
            pltpu.VMEM((around, pairs * HALVES, LANES), jnp.float32),
            pltpu.VMEM((around * cells * HALVES, LANES), jnp.float32),
            pltpu.VMEM((groups, cells * 3 * HALVES, LANES), jnp.float32),
            pltpu.VMEM((cells * HALVES, LANES), jnp.float32),
            pltpu.VMEM((pairs, HALVES, CELL, LANES), jnp.float32),
            pltpu.VMEM((pairs, 3 * HALVES, CELL, LANES), jnp.float32),
            pltpu.VMEM((pairs, 4 * HALVES, LANES), jnp.float32),
            pltpu.SemaphoreType.DMA((5,)),
            pltpu.SemaphoreType.DMA((2,)),
            pltpu.SemaphoreType.DMA((2,)),
            pltpu.SemaphoreType.DMA((2,)),
            pltpu.SemaphoreType.DMA((2,)),
            pltpu.SemaphoreType.DMA((2,)),
        ],
        compiler_params=pltpu.CompilerParams(
            collective_id=0, has_side_effects=True, vmem_limit_bytes=64 * 1024 * 1024
        ),
    )(tasks, counts, positions, mass[None], smooth[None])
    return pl.pallas_call(
        deliver,
        out_shape=(
            jax.ShapeDtypeStruct(mass.shape, jnp.float32),
            jax.ShapeDtypeStruct(positions.shape, jnp.float32),
        ),
        in_specs=[hbm] * 2,
        out_specs=(hbm, hbm),
        scratch_shapes=[
            pltpu.VMEM(mass.shape, jnp.float32),
            pltpu.VMEM(forces.shape, jnp.float32),
            pltpu.VMEM(positions.shape, jnp.float32),
            pltpu.SemaphoreType.DMA((4,)),
        ],
        compiler_params=pltpu.CompilerParams(vmem_limit_bytes=64 * 1024 * 1024),
    )(density.reshape(-1), forces)


def solution(mesh):
    in_specs = (
        P(None, ("dom", "grp")),
        P(("dom", "grp")),
        P(("dom", "grp")),
        P(("dom", "grp")),
        P(None, ("dom", "grp")),
    )
    out_specs = (P(("dom", "grp")), P(None, ("dom", "grp")))
    return jax.shard_map(local, mesh=mesh, in_specs=in_specs, out_specs=out_specs, check_vma=False)
```

```python
import functools
import math

import jax
import jax.numpy as jnp
from jax import lax
from jax.experimental import pallas as pl
from jax.experimental.pallas import tpu as pltpu
from jax.sharding import PartitionSpec as P

CELL = 256
LANES = 128
HALVES = CELL // LANES
CHUNK = 32
MESH = pl.DeviceIdType.MESH
DENSITY_SCALE = 21.0 / (2.0 * math.pi)
FORCE_SCALE = 105.0 / math.pi


def kernel(
    doms, groups, cells, pairs, tasks_hbm, counts_hbm, pos_hbm, mass_hbm, smooth_hbm,
    rho_out, forces,
    tasks_ref, counts_ref, pos_ref, mass_ref, smooth_ref,
    pool, tail, slab_tail, parts, rho, to_owner, rho_own, weights, waiting, early,
    in_sem, main_sem, near_sem, far_sem, parts_sem, force_sem,
):
    slab_cells = groups * cells
    dom = lax.axis_index("dom")
    member = lax.axis_index("grp")
    own = groups + member
    around = 3 * groups

    def place(e, z):
        return (lax.rem(dom + e + doms, doms), z)

    def each_far(act):
        def step(i, carry):
            act(2 * lax.div(i, groups) - 1, lax.rem(member + i, groups), i)
            return carry

        lax.fori_loop(0, 2 * groups, step, 0)

    def each_near(act):
        def step(g, carry):
            act(0, lax.rem(member + g, groups), 2 * groups + g)
            return carry

        lax.fori_loop(1, groups, step, 0)

    def each(act):
        each_far(act)
        each_near(act)

    def start(ref, sems):
        def copy(e, z, n):
            slot = (1 - e) * groups + member
            pltpu.make_async_remote_copy(
                src_ref=ref.at[own], dst_ref=ref.at[slot], send_sem=sems.at[0], recv_sem=sems.at[1],
                device_id=place(e, z), device_id_type=MESH,
            ).start()

        return copy

    def whole(ref, sems, count):
        return pltpu.make_async_remote_copy(
            src_ref=ref.at[pl.ds(0, count)], dst_ref=ref.at[pl.ds(0, count)], send_sem=sems.at[0],
            recv_sem=sems.at[1], device_id=place(0, lax.rem(member + 1, groups)), device_id_type=MESH,
        )

    barrier = pltpu.get_barrier_semaphore()
    each(lambda e, z, n: pl.semaphore_signal(barrier, inc=1, device_id=place(e, z), device_id_type=MESH))
    moves = (
        (tasks_hbm, tasks_ref), (counts_hbm, counts_ref), (pos_hbm, pos_ref), (mass_hbm, mass_ref),
        (smooth_hbm, smooth_ref),
    )
    inputs = [pltpu.make_async_copy(*move, in_sem.at[n]) for n, move in enumerate(moves)]
    for copy in inputs:
        copy.start()
    for copy in inputs:
        copy.wait()

    lane = lax.broadcasted_iota(jnp.int32, (1, LANES), 1)
    for c in range(cells):
        for h in range(HALVES):
            at = pl.ds(c * CELL + h * LANES, LANES)
            live = (lane + h * LANES < counts_ref[c]).astype(jnp.float32)
            for d in range(3):
                pool[own, c, pl.ds(d * HALVES + h, 1), :] = pos_ref[pl.ds(d, 1), at]
            pool[own, c, pl.ds(3 * HALVES + h, 1), :] = mass_ref[:, at] * live
            tail[own, pl.ds(c * HALVES + h, 1), :] = smooth_ref[:, at]
    for t in range(pairs):
        tail[own, pl.ds(cells * HALVES + t, 1), :] = jnp.full((1, LANES), tasks_ref[0, t]).astype(jnp.float32)

    pl.semaphore_wait(barrier, around - 1)
    each_near(start(tail, near_sem))
    each(start(pool, main_sem))
    whole(pool, main_sem, around - 1).wait_recv()
    whole(tail, near_sem, groups - 1).wait_recv()
    slab_tail[...] = tail[pl.ds(groups, groups)]

    def receiver(slot, cell):
        block = pool[slot, cell]
        lengths = slab_tail[slot - groups]
        length = lengths[0:HALVES]
        for c in range(1, cells):
            length = jnp.where(cell == c, lengths[c * HALVES:(c + 1) * HALVES], length)
        inverse = 1.0 / length
        rows = []
        for h in range(HALVES):
            rows.append([block[d * HALVES + h:d * HALVES + h + 1] for d in range(3)] + [inverse[h:h + 1], block[3 * HALVES + h:3 * HALVES + h + 1]])
        return rows

    def chunks(source):
        for s in range(HALVES):
            for q in range(0, LANES, CHUNK):
                yield s, q, [source[q:q + CHUNK, d * HALVES + s:d * HALVES + s + 1] for d in range(4)]

    def inside(row, col):
        diffs = [row[d] - col[d] for d in range(3)]
        square = (diffs[0] * diffs[0] + diffs[1] * diffs[1] + diffs[2] * diffs[2]) * (row[3] * row[3])
        ratio = square * lax.rsqrt(jnp.maximum(square, 1e-30))
        return jnp.maximum(1.0 - ratio, 0.0)

    def task(t):
        recv, k = tasks_ref[0, t], tasks_ref[1, t]
        rows = receiver(groups + recv // cells, lax.rem(recv, cells))
        return rows, jnp.transpose(pool[k // cells, lax.rem(k, cells)])

    for t in range(pairs):
        rows, source = task(t)
        total = [jnp.zeros((CHUNK, LANES), jnp.float32) for _ in range(HALVES)]
        for s, q, col in chunks(source):
            for h in range(HALVES):
                u = inside(rows[h], col)
                u2 = u * u
                heavy = u2 * col[3]
                weights[t, h, pl.ds(s * LANES + q, CHUNK), :] = heavy * u
                total[h] = total[h] + (heavy * u2) * (1.25 - u)
        for h in range(HALVES):
            value = jnp.sum(total[h], axis=0, keepdims=True)
            inv = rows[h][3]
            parts[own, pl.ds(t * HALVES + h, 1), :] = value * (inv * inv * inv) * (4.0 * DENSITY_SCALE)
    each(start(parts, parts_sem))
    each_far(start(tail, far_sem))

    def prepare(t, carry):
        rows, source = task(t)
        total = [[jnp.zeros((CHUNK, LANES), jnp.float32) for _ in range(3)] for _ in range(HALVES)]
        for s, q, col in chunks(source):
            for h in range(HALVES):
                weight = weights[t, h, pl.ds(s * LANES + q, CHUNK), :]
                for d in range(3):
                    term = weight * (rows[h][d] - col[d])
                    waiting[t, d * HALVES + h, pl.ds(s * LANES + q, CHUNK), :] = term
                    total[h][d] = total[h][d] + term
        for h in range(HALVES):
            inv = rows[h][3]
            fifth = FORCE_SCALE * (inv * inv) * (inv * inv) * inv
            early[t, pl.ds(3 * HALVES + h, 1), :] = jnp.where(rows[h][4] > 0.0, fifth, 0.0)
            for d in range(3):
                early[t, pl.ds(d * HALVES + h, 1), :] = jnp.sum(total[h][d], axis=0, keepdims=True)
        return carry

    lax.fori_loop(0, pairs, prepare, 0)

    whole(tail, far_sem, 2 * groups).wait_recv()
    for slot in range(3 * groups):
        for c in range(cells):
            m = pool[slot, c, pl.ds(3 * HALVES, HALVES), :]
            inv = 1.0 / tail[slot, pl.ds(c * HALVES, HALVES), :]
            rho[pl.ds((slot * cells + c) * HALVES, HALVES), :] = m * (inv * inv * inv) * DENSITY_SCALE

    whole(parts, parts_sem, around - 1).wait_recv()

    span = slab_cells * HALVES
    index = lax.broadcasted_iota(jnp.int32, (span, LANES), 0)
    odd = lax.rem(index, HALVES)
    cell_of = (index // HALVES).astype(jnp.float32)
    for d in range(3):
        total = rho[pl.ds(d * span, span), :]
        for g in range(groups):
            slot = d * groups + g
            part = parts[slot]
            to = tail[slot]
            for t in range(pairs):
                value = part[t * HALVES:t * HALVES + 1]
                for h in range(1, HALVES):
                    value = jnp.where(odd == h, part[t * HALVES + h:t * HALVES + h + 1], value)
                at = to[cells * HALVES + t:cells * HALVES + t + 1]
                total = total + jnp.where(cell_of == at, value, 0.0)
        rho[pl.ds(d * span, span), :] = total

    source_rho = [rho[pl.ds(tasks_ref[1, t] * HALVES, HALVES), :] for t in range(pairs)]
    source_rho = 1.0 / jnp.maximum(jnp.concatenate(source_rho, axis=0), 1e-30)
    columns = jnp.transpose(source_rho)
    to_cell = [None] * slab_cells
    for t in range(pairs):
        recv = tasks_ref[0, t]
        a_rho = 1.0 / jnp.maximum(rho[pl.ds((slab_cells + recv) * HALVES, HALVES), :], 1e-30)
        total = [[jnp.zeros((CHUNK, LANES), jnp.float32) for _ in range(3)] for _ in range(HALVES)]
        for s in range(HALVES):
            for q in range(0, LANES, CHUNK):
                col = columns[q:q + CHUNK, t * HALVES + s:t * HALVES + s + 1]
                for h in range(HALVES):
                    for d in range(3):
                        term = waiting[t, d * HALVES + h, pl.ds(s * LANES + q, CHUNK), :]
                        total[h][d] = total[h][d] + term * col
        sums = []
        for d in range(3):
            for h in range(HALVES):
                at = pl.ds(d * HALVES + h, 1)
                value = jnp.sum(total[h][d], axis=0, keepdims=True) + early[t, at, :] * a_rho[h:h + 1]
                sums.append(value * early[t, pl.ds(3 * HALVES + h, 1), :])
        sums = jnp.concatenate(sums, axis=0)
        for cell in range(slab_cells):
            value = jnp.where(recv == cell, sums, 0.0)
            to_cell[cell] = value if t == 0 else to_cell[cell] + value

    rows = 3 * HALVES
    for cell in range(slab_cells):
        to_owner[cell // cells, pl.ds(cell % cells * rows, rows), :] = to_cell[cell]

    def owner_copy(e, z, n):
        pltpu.make_async_remote_copy(
            src_ref=to_owner.at[z], dst_ref=forces.at[member], send_sem=force_sem.at[0], recv_sem=force_sem.at[1],
            device_id=place(0, z), device_id_type=MESH,
        ).start()

    each_near(owner_copy)

    for c in range(cells):
        for h in range(HALVES):
            live = (lane + h * LANES < counts_ref[c]).astype(jnp.float32)
            rho_own[pl.ds(c * HALVES + h, 1), :] = rho[pl.ds((own * cells + c) * HALVES + h, 1), :] * live
    outs = [
        pltpu.make_async_copy(to_owner.at[member], forces.at[member], in_sem.at[0]),
        pltpu.make_async_copy(rho_own, rho_out, in_sem.at[1]),
    ]
    for copy in outs:
        copy.start()

    whole(pool, main_sem, around - 1).wait_send()
    whole(tail, near_sem, groups - 1).wait_send()
    whole(tail, far_sem, 2 * groups).wait_send()
    whole(parts, parts_sem, around - 1).wait_send()
    for copy in outs:
        copy.wait()
    whole(forces, force_sem, groups - 1).wait_recv()
    whole(to_owner, force_sem, groups - 1).wait_send()


def deliver(density_hbm, forces_hbm, density_out, accel_out, density, forces, accel, sems):
    ins = [
        pltpu.make_async_copy(density_hbm, density, sems.at[0]),
        pltpu.make_async_copy(forces_hbm, forces, sems.at[1]),
    ]
    for copy in ins:
        copy.start()
    ins[0].wait()
    outs = [pltpu.make_async_copy(density, density_out, sems.at[2])]
    outs[0].start()
    ins[1].wait()
    total = forces[0]
    for g in range(1, forces.shape[0]):
        total = total + forces[g]
    for at in range(total.shape[0]):
        c, d, h = at // (3 * HALVES), at // HALVES % 3, at % HALVES
        accel[pl.ds(d, 1), pl.ds(c * CELL + h * LANES, LANES)] = total[at:at + 1]
    outs.append(pltpu.make_async_copy(accel, accel_out, sems.at[3]))
    outs[1].start()
    for copy in outs:
        copy.wait()


def local(positions, mass, smooth, counts, tasks):
    groups, doms = lax.axis_size("grp"), lax.axis_size("dom")
    cells, pairs = counts.shape[0], tasks.shape[1]
    around = 3 * groups
    last = max(8, -(-(cells * HALVES + pairs) // 8) * 8)
    hbm = pl.BlockSpec(memory_space=pltpu.HBM)
    density, forces = pl.pallas_call(
        functools.partial(kernel, doms, groups, cells, pairs),
        out_shape=(
            jax.ShapeDtypeStruct((cells * HALVES, LANES), jnp.float32),
            jax.ShapeDtypeStruct((groups, cells * 3 * HALVES, LANES), jnp.float32),
        ),
        in_specs=[hbm] * 5,
        out_specs=(hbm, hbm),
        scratch_shapes=[
            pltpu.SMEM(tasks.shape, jnp.int32),
            pltpu.SMEM(counts.shape, jnp.int32),
            pltpu.VMEM(positions.shape, jnp.float32),
            pltpu.VMEM((1, mass.shape[0]), jnp.float32),
            pltpu.VMEM((1, smooth.shape[0]), jnp.float32),
            pltpu.VMEM((around, cells, 4 * HALVES, LANES), jnp.float32),
            pltpu.VMEM((around, last, LANES), jnp.float32),
            pltpu.VMEM((groups, last, LANES), jnp.float32),
            pltpu.VMEM((around, pairs * HALVES, LANES), jnp.float32),
            pltpu.VMEM((around * cells * HALVES, LANES), jnp.float32),
            pltpu.VMEM((groups, cells * 3 * HALVES, LANES), jnp.float32),
            pltpu.VMEM((cells * HALVES, LANES), jnp.float32),
            pltpu.VMEM((pairs, HALVES, CELL, LANES), jnp.float32),
            pltpu.VMEM((pairs, 3 * HALVES, CELL, LANES), jnp.float32),
            pltpu.VMEM((pairs, 4 * HALVES, LANES), jnp.float32),
            pltpu.SemaphoreType.DMA((5,)),
            pltpu.SemaphoreType.DMA((2,)),
            pltpu.SemaphoreType.DMA((2,)),
            pltpu.SemaphoreType.DMA((2,)),
            pltpu.SemaphoreType.DMA((2,)),
            pltpu.SemaphoreType.DMA((2,)),
        ],
        compiler_params=pltpu.CompilerParams(
            collective_id=0, has_side_effects=True, vmem_limit_bytes=64 * 1024 * 1024
        ),
    )(tasks, counts, positions, mass[None], smooth[None])
    return pl.pallas_call(
        deliver,
        out_shape=(
            jax.ShapeDtypeStruct(mass.shape, jnp.float32),
            jax.ShapeDtypeStruct(positions.shape, jnp.float32),
        ),
        in_specs=[hbm] * 2,
        out_specs=(hbm, hbm),
        scratch_shapes=[
            pltpu.VMEM(mass.shape, jnp.float32),
            pltpu.VMEM(forces.shape, jnp.float32),
            pltpu.VMEM(positions.shape, jnp.float32),
            pltpu.SemaphoreType.DMA((4,)),
        ],
        compiler_params=pltpu.CompilerParams(vmem_limit_bytes=64 * 1024 * 1024),
    )(density.reshape(-1), forces)


def solution(mesh):
    in_specs = (
        P(None, ("dom", "grp")),
        P(("dom", "grp")),
        P(("dom", "grp")),
        P(("dom", "grp")),
        P(None, ("dom", "grp")),
    )
    out_specs = (P(("dom", "grp")), P(None, ("dom", "grp")))
    return jax.shard_map(local, mesh=mesh, in_specs=in_specs, out_specs=out_specs, check_vma=False)
```

```python
import functools
import math

import jax
import jax.numpy as jnp
from jax import lax
from jax.experimental import pallas as pl
from jax.experimental.pallas import tpu as pltpu
from jax.sharding import PartitionSpec as P

CELL = 256
LANES = 128
HALVES = CELL // LANES
CHUNK = 16
MESH = pl.DeviceIdType.MESH
DENSITY_SCALE = 21.0 / (2.0 * math.pi)
FORCE_SCALE = 105.0 / math.pi


def kernel(
    doms, groups, cells, pairs, tasks_hbm, counts_hbm, pos_hbm, mass_hbm, smooth_hbm,
    rho_out, forces,
    tasks_ref, counts_ref, pos_ref, mass_ref, smooth_ref,
    pool, tail, slab_tail, parts, rho, to_owner, rho_own, weights, waiting, early,
    in_sem, main_sem, near_sem, far_sem, parts_sem, force_sem,
):
    slab_cells = groups * cells
    dom = lax.axis_index("dom")
    member = lax.axis_index("grp")
    own = groups + member
    around = 3 * groups

    def place(e, z):
        return (lax.rem(dom + e + doms, doms), z)

    def each_far(act):
        def step(i, carry):
            act(2 * lax.div(i, groups) - 1, lax.rem(member + i, groups), i)
            return carry

        lax.fori_loop(0, 2 * groups, step, 0)

    def each_near(act):
        def step(g, carry):
            act(0, lax.rem(member + g, groups), 2 * groups + g)
            return carry

        lax.fori_loop(1, groups, step, 0)

    def each(act):
        each_far(act)
        each_near(act)

    def start(ref, sems):
        def copy(e, z, n):
            slot = (1 - e) * groups + member
            pltpu.make_async_remote_copy(
                src_ref=ref.at[own], dst_ref=ref.at[slot], send_sem=sems.at[0], recv_sem=sems.at[1],
                device_id=place(e, z), device_id_type=MESH,
            ).start()

        return copy

    def whole(ref, sems, count):
        return pltpu.make_async_remote_copy(
            src_ref=ref.at[pl.ds(0, count)], dst_ref=ref.at[pl.ds(0, count)], send_sem=sems.at[0],
            recv_sem=sems.at[1], device_id=place(0, lax.rem(member + 1, groups)), device_id_type=MESH,
        )

    barrier = pltpu.get_barrier_semaphore()
    each(lambda e, z, n: pl.semaphore_signal(barrier, inc=1, device_id=place(e, z), device_id_type=MESH))
    moves = (
        (tasks_hbm, tasks_ref), (counts_hbm, counts_ref), (pos_hbm, pos_ref), (mass_hbm, mass_ref),
        (smooth_hbm, smooth_ref),
    )
    inputs = [pltpu.make_async_copy(*move, in_sem.at[n]) for n, move in enumerate(moves)]
    for copy in inputs:
        copy.start()
    for copy in inputs:
        copy.wait()

    lane = lax.broadcasted_iota(jnp.int32, (1, LANES), 1)
    for c in range(cells):
        for h in range(HALVES):
            at = pl.ds(c * CELL + h * LANES, LANES)
            live = (lane + h * LANES < counts_ref[c]).astype(jnp.float32)
            for d in range(3):
                pool[own, c, pl.ds(d * HALVES + h, 1), :] = pos_ref[pl.ds(d, 1), at]
            pool[own, c, pl.ds(3 * HALVES + h, 1), :] = mass_ref[:, at] * live
            tail[own, pl.ds(c * HALVES + h, 1), :] = smooth_ref[:, at]
    for t in range(pairs):
        tail[own, pl.ds(cells * HALVES + t, 1), :] = jnp.full((1, LANES), tasks_ref[0, t]).astype(jnp.float32)

    pl.semaphore_wait(barrier, around - 1)
    each(start(pool, main_sem))
    each_near(start(tail, near_sem))
    each_far(start(tail, far_sem))
    whole(pool, main_sem, around - 1).wait_recv()
    whole(tail, near_sem, groups - 1).wait_recv()
    slab_tail[...] = tail[pl.ds(groups, groups)]

    def receiver(slot, cell):
        block = pool[slot, cell]
        lengths = slab_tail[slot - groups]
        length = lengths[0:HALVES]
        for c in range(1, cells):
            length = jnp.where(cell == c, lengths[c * HALVES:(c + 1) * HALVES], length)
        inverse = 1.0 / length
        rows = []
        for h in range(HALVES):
            rows.append([block[d * HALVES + h:d * HALVES + h + 1] for d in range(3)] + [inverse[h:h + 1], block[3 * HALVES + h:3 * HALVES + h + 1]])
        return rows

    def chunks(source):
        for s in range(HALVES):
            for q in range(0, LANES, CHUNK):
                yield s, q, [source[q:q + CHUNK, d * HALVES + s:d * HALVES + s + 1] for d in range(4)]

    def inside(row, col):
        diffs = [row[d] - col[d] for d in range(3)]
        square = (diffs[0] * diffs[0] + diffs[1] * diffs[1] + diffs[2] * diffs[2]) * (row[3] * row[3])
        ratio = square * lax.rsqrt(jnp.maximum(square, 1e-30))
        return jnp.maximum(1.0 - ratio, 0.0)

    def task(t):
        recv, k = tasks_ref[0, t], tasks_ref[1, t]
        rows = receiver(groups + recv // cells, lax.rem(recv, cells))
        return rows, jnp.transpose(pool[k // cells, lax.rem(k, cells)])

    for t in range(pairs):
        rows, source = task(t)
        total = [jnp.zeros((CHUNK, LANES), jnp.float32) for _ in range(HALVES)]
        for s, q, col in chunks(source):
            for h in range(HALVES):
                u = inside(rows[h], col)
                u2 = u * u
                heavy = u2 * col[3]
                weights[t, h, pl.ds(s * LANES + q, CHUNK), :] = heavy * u
                total[h] = total[h] + (heavy * u2) * (1.25 - u)
        for h in range(HALVES):
            value = jnp.sum(total[h], axis=0, keepdims=True)
            inv = rows[h][3]
            parts[own, pl.ds(t * HALVES + h, 1), :] = value * (inv * inv * inv) * (4.0 * DENSITY_SCALE)
    each(start(parts, parts_sem))

    def prepare(t, carry):
        rows, source = task(t)
        total = [[jnp.zeros((CHUNK, LANES), jnp.float32) for _ in range(3)] for _ in range(HALVES)]
        for s, q, col in chunks(source):
            for h in range(HALVES):
                weight = weights[t, h, pl.ds(s * LANES + q, CHUNK), :]
                for d in range(3):
                    term = weight * (rows[h][d] - col[d])
                    waiting[t, d * HALVES + h, pl.ds(s * LANES + q, CHUNK), :] = term
                    total[h][d] = total[h][d] + term
        for h in range(HALVES):
            inv = rows[h][3]
            fifth = FORCE_SCALE * (inv * inv) * (inv * inv) * inv
            early[t, pl.ds(3 * HALVES + h, 1), :] = jnp.where(rows[h][4] > 0.0, fifth, 0.0)
            for d in range(3):
                early[t, pl.ds(d * HALVES + h, 1), :] = jnp.sum(total[h][d], axis=0, keepdims=True)
        return carry

    lax.fori_loop(0, pairs, prepare, 0)

    whole(tail, far_sem, 2 * groups).wait_recv()
    for slot in range(3 * groups):
        for c in range(cells):
            m = pool[slot, c, pl.ds(3 * HALVES, HALVES), :]
            inv = 1.0 / tail[slot, pl.ds(c * HALVES, HALVES), :]
            rho[pl.ds((slot * cells + c) * HALVES, HALVES), :] = m * (inv * inv * inv) * DENSITY_SCALE

    whole(parts, parts_sem, around - 1).wait_recv()

    span = slab_cells * HALVES
    index = lax.broadcasted_iota(jnp.int32, (span, LANES), 0)
    odd = lax.rem(index, HALVES)
    cell_of = (index // HALVES).astype(jnp.float32)
    for d in range(3):
        total = rho[pl.ds(d * span, span), :]
        for g in range(groups):
            slot = d * groups + g
            part = parts[slot]
            to = tail[slot]
            for t in range(pairs):
                value = part[t * HALVES:t * HALVES + 1]
                for h in range(1, HALVES):
                    value = jnp.where(odd == h, part[t * HALVES + h:t * HALVES + h + 1], value)
                at = to[cells * HALVES + t:cells * HALVES + t + 1]
                total = total + jnp.where(cell_of == at, value, 0.0)
        rho[pl.ds(d * span, span), :] = total

    source_rho = [rho[pl.ds(tasks_ref[1, t] * HALVES, HALVES), :] for t in range(pairs)]
    source_rho = 1.0 / jnp.maximum(jnp.concatenate(source_rho, axis=0), 1e-30)
    columns = jnp.transpose(source_rho)
    to_cell = [None] * slab_cells
    for t in range(pairs):
        recv = tasks_ref[0, t]
        a_rho = 1.0 / jnp.maximum(rho[pl.ds((slab_cells + recv) * HALVES, HALVES), :], 1e-30)
        total = [[jnp.zeros((CHUNK, LANES), jnp.float32) for _ in range(3)] for _ in range(HALVES)]
        for s in range(HALVES):
            for q in range(0, LANES, CHUNK):
                col = columns[q:q + CHUNK, t * HALVES + s:t * HALVES + s + 1]
                for h in range(HALVES):
                    for d in range(3):
                        term = waiting[t, d * HALVES + h, pl.ds(s * LANES + q, CHUNK), :]
                        total[h][d] = total[h][d] + term * col
        sums = []
        for d in range(3):
            for h in range(HALVES):
                at = pl.ds(d * HALVES + h, 1)
                value = jnp.sum(total[h][d], axis=0, keepdims=True) + early[t, at, :] * a_rho[h:h + 1]
                sums.append(value * early[t, pl.ds(3 * HALVES + h, 1), :])
        sums = jnp.concatenate(sums, axis=0)
        for cell in range(slab_cells):
            value = jnp.where(recv == cell, sums, 0.0)
            to_cell[cell] = value if t == 0 else to_cell[cell] + value

    rows = 3 * HALVES
    for cell in range(slab_cells):
        to_owner[cell // cells, pl.ds(cell % cells * rows, rows), :] = to_cell[cell]

    def owner_copy(e, z, n):
        pltpu.make_async_remote_copy(
            src_ref=to_owner.at[z], dst_ref=forces.at[member], send_sem=force_sem.at[0], recv_sem=force_sem.at[1],
            device_id=place(0, z), device_id_type=MESH,
        ).start()

    each_near(owner_copy)

    for c in range(cells):
        for h in range(HALVES):
            live = (lane + h * LANES < counts_ref[c]).astype(jnp.float32)
            rho_own[pl.ds(c * HALVES + h, 1), :] = rho[pl.ds((own * cells + c) * HALVES + h, 1), :] * live
    outs = [
        pltpu.make_async_copy(to_owner.at[member], forces.at[member], in_sem.at[0]),
        pltpu.make_async_copy(rho_own, rho_out, in_sem.at[1]),
    ]
    for copy in outs:
        copy.start()

    whole(pool, main_sem, around - 1).wait_send()
    whole(tail, near_sem, groups - 1).wait_send()
    whole(tail, far_sem, 2 * groups).wait_send()
    whole(parts, parts_sem, around - 1).wait_send()
    for copy in outs:
        copy.wait()
    whole(forces, force_sem, groups - 1).wait_recv()
    whole(to_owner, force_sem, groups - 1).wait_send()


def deliver(density_hbm, forces_hbm, density_out, accel_out, density, forces, accel, sems):
    ins = [
        pltpu.make_async_copy(density_hbm, density, sems.at[0]),
        pltpu.make_async_copy(forces_hbm, forces, sems.at[1]),
    ]
    for copy in ins:
        copy.start()
    ins[0].wait()
    outs = [pltpu.make_async_copy(density, density_out, sems.at[2])]
    outs[0].start()
    ins[1].wait()
    total = forces[0]
    for g in range(1, forces.shape[0]):
        total = total + forces[g]
    for at in range(total.shape[0]):
        c, d, h = at // (3 * HALVES), at // HALVES % 3, at % HALVES
        accel[pl.ds(d, 1), pl.ds(c * CELL + h * LANES, LANES)] = total[at:at + 1]
    outs.append(pltpu.make_async_copy(accel, accel_out, sems.at[3]))
    outs[1].start()
    for copy in outs:
        copy.wait()


def local(positions, mass, smooth, counts, tasks):
    groups, doms = lax.axis_size("grp"), lax.axis_size("dom")
    cells, pairs = counts.shape[0], tasks.shape[1]
    around = 3 * groups
    last = max(8, -(-(cells * HALVES + pairs) // 8) * 8)
    hbm = pl.BlockSpec(memory_space=pltpu.HBM)
    density, forces = pl.pallas_call(
        functools.partial(kernel, doms, groups, cells, pairs),
        out_shape=(
            jax.ShapeDtypeStruct((cells * HALVES, LANES), jnp.float32),
            jax.ShapeDtypeStruct((groups, cells * 3 * HALVES, LANES), jnp.float32),
        ),
        in_specs=[hbm] * 5,
        out_specs=(hbm, hbm),
        scratch_shapes=[
            pltpu.SMEM(tasks.shape, jnp.int32),
            pltpu.SMEM(counts.shape, jnp.int32),
            pltpu.VMEM(positions.shape, jnp.float32),
            pltpu.VMEM((1, mass.shape[0]), jnp.float32),
            pltpu.VMEM((1, smooth.shape[0]), jnp.float32),
            pltpu.VMEM((around, cells, 4 * HALVES, LANES), jnp.float32),
            pltpu.VMEM((around, last, LANES), jnp.float32),
            pltpu.VMEM((groups, last, LANES), jnp.float32),
            pltpu.VMEM((around, pairs * HALVES, LANES), jnp.float32),
            pltpu.VMEM((around * cells * HALVES, LANES), jnp.float32),
            pltpu.VMEM((groups, cells * 3 * HALVES, LANES), jnp.float32),
            pltpu.VMEM((cells * HALVES, LANES), jnp.float32),
            pltpu.VMEM((pairs, HALVES, CELL, LANES), jnp.float32),
            pltpu.VMEM((pairs, 3 * HALVES, CELL, LANES), jnp.float32),
            pltpu.VMEM((pairs, 4 * HALVES, LANES), jnp.float32),
            pltpu.SemaphoreType.DMA((5,)),
            pltpu.SemaphoreType.DMA((2,)),
            pltpu.SemaphoreType.DMA((2,)),
            pltpu.SemaphoreType.DMA((2,)),
            pltpu.SemaphoreType.DMA((2,)),
            pltpu.SemaphoreType.DMA((2,)),
        ],
        compiler_params=pltpu.CompilerParams(
            collective_id=0, has_side_effects=True, vmem_limit_bytes=64 * 1024 * 1024
        ),
    )(tasks, counts, positions, mass[None], smooth[None])
    return pl.pallas_call(
        deliver,
        out_shape=(
            jax.ShapeDtypeStruct(mass.shape, jnp.float32),
            jax.ShapeDtypeStruct(positions.shape, jnp.float32),
        ),
        in_specs=[hbm] * 2,
        out_specs=(hbm, hbm),
        scratch_shapes=[
            pltpu.VMEM(mass.shape, jnp.float32),
            pltpu.VMEM(forces.shape, jnp.float32),
            pltpu.VMEM(positions.shape, jnp.float32),
            pltpu.SemaphoreType.DMA((4,)),
        ],
        compiler_params=pltpu.CompilerParams(vmem_limit_bytes=64 * 1024 * 1024),
    )(density.reshape(-1), forces)


def solution(mesh):
    in_specs = (
        P(None, ("dom", "grp")),
        P(("dom", "grp")),
        P(("dom", "grp")),
        P(("dom", "grp")),
        P(None, ("dom", "grp")),
    )
    out_specs = (P(("dom", "grp")), P(None, ("dom", "grp")))
    return jax.shard_map(local, mesh=mesh, in_specs=in_specs, out_specs=out_specs, check_vma=False)
```

```python
import functools
import math

import jax
import jax.numpy as jnp
from jax import lax
from jax.experimental import pallas as pl
from jax.experimental.pallas import tpu as pltpu
from jax.sharding import PartitionSpec as P

CELL = 256
LANES = 128
HALVES = CELL // LANES
CHUNK = 32
MESH = pl.DeviceIdType.MESH
DENSITY_SCALE = 21.0 / (2.0 * math.pi)
FORCE_SCALE = 105.0 / math.pi


def kernel(
    doms, groups, cells, pairs, tasks_hbm, counts_hbm, pos_hbm, mass_hbm, smooth_hbm,
    rho_out, forces,
    tasks_ref, counts_ref, pos_ref, mass_ref, smooth_ref,
    pool, tail, slab_tail, parts, rho, to_owner, rho_own, weights, waiting, early,
    in_sem, main_sem, near_sem, far_sem, parts_sem, force_sem,
):
    slab_cells = groups * cells
    dom = lax.axis_index("dom")
    member = lax.axis_index("grp")
    own = groups + member
    around = 3 * groups

    def place(e, z):
        return (lax.rem(dom + e + doms, doms), z)

    def each_far(act):
        def step(i, carry):
            act(2 * lax.rem(i, 2) - 1, lax.rem(member + 1 + lax.div(i, 2), groups), i)
            return carry

        lax.fori_loop(0, 2 * groups, step, 0)

    def each_near(act):
        def step(g, carry):
            act(0, lax.rem(member + g, groups), 2 * groups + g)
            return carry

        lax.fori_loop(1, groups, step, 0)

    def each(act):
        each_far(act)
        each_near(act)

    def start(ref, sems):
        def copy(e, z, n):
            slot = (1 - e) * groups + member
            pltpu.make_async_remote_copy(
                src_ref=ref.at[own], dst_ref=ref.at[slot], send_sem=sems.at[0], recv_sem=sems.at[1],
                device_id=place(e, z), device_id_type=MESH,
            ).start()

        return copy

    def whole(ref, sems, count):
        return pltpu.make_async_remote_copy(
            src_ref=ref.at[pl.ds(0, count)], dst_ref=ref.at[pl.ds(0, count)], send_sem=sems.at[0],
            recv_sem=sems.at[1], device_id=place(0, lax.rem(member + 1, groups)), device_id_type=MESH,
        )

    barrier = pltpu.get_barrier_semaphore()
    each(lambda e, z, n: pl.semaphore_signal(barrier, inc=1, device_id=place(e, z), device_id_type=MESH))
    moves = (
        (tasks_hbm, tasks_ref), (counts_hbm, counts_ref), (pos_hbm, pos_ref), (mass_hbm, mass_ref),
        (smooth_hbm, smooth_ref),
    )
    inputs = [pltpu.make_async_copy(*move, in_sem.at[n]) for n, move in enumerate(moves)]
    for copy in inputs:
        copy.start()
    for copy in inputs:
        copy.wait()

    lane = lax.broadcasted_iota(jnp.int32, (1, LANES), 1)
    for c in range(cells):
        for h in range(HALVES):
            at = pl.ds(c * CELL + h * LANES, LANES)
            live = (lane + h * LANES < counts_ref[c]).astype(jnp.float32)
            for d in range(3):
                pool[own, c, pl.ds(d * HALVES + h, 1), :] = pos_ref[pl.ds(d, 1), at]
            pool[own, c, pl.ds(3 * HALVES + h, 1), :] = mass_ref[:, at] * live
            tail[own, pl.ds(c * HALVES + h, 1), :] = smooth_ref[:, at]
    for t in range(pairs):
        tail[own, pl.ds(cells * HALVES + t, 1), :] = jnp.full((1, LANES), tasks_ref[0, t]).astype(jnp.float32)

    pl.semaphore_wait(barrier, around - 1)
    each(start(pool, main_sem))
    each_near(start(tail, near_sem))
    each_far(start(tail, far_sem))
    whole(pool, main_sem, around - 1).wait_recv()
    whole(tail, near_sem, groups - 1).wait_recv()
    slab_tail[...] = tail[pl.ds(groups, groups)]

    def receiver(slot, cell):
        block = pool[slot, cell]
        lengths = slab_tail[slot - groups]
        length = lengths[0:HALVES]
        for c in range(1, cells):
            length = jnp.where(cell == c, lengths[c * HALVES:(c + 1) * HALVES], length)
        inverse = 1.0 / length
        rows = []
        for h in range(HALVES):
            rows.append([block[d * HALVES + h:d * HALVES + h + 1] for d in range(3)] + [inverse[h:h + 1], block[3 * HALVES + h:3 * HALVES + h + 1]])
        return rows

    def chunks(source):
        for s in range(HALVES):
            for q in range(0, LANES, CHUNK):
                yield s, q, [source[q:q + CHUNK, d * HALVES + s:d * HALVES + s + 1] for d in range(4)]

    def inside(row, col):
        diffs = [row[d] - col[d] for d in range(3)]
        square = (diffs[0] * diffs[0] + diffs[1] * diffs[1] + diffs[2] * diffs[2]) * (row[3] * row[3])
        ratio = square * lax.rsqrt(jnp.maximum(square, 1e-30))
        return jnp.maximum(1.0 - ratio, 0.0)

    def task(t):
        recv, k = tasks_ref[0, t], tasks_ref[1, t]
        rows = receiver(groups + recv // cells, lax.rem(recv, cells))
        return rows, jnp.transpose(pool[k // cells, lax.rem(k, cells)])

    for t in range(pairs):
        rows, source = task(t)
        total = [jnp.zeros((CHUNK, LANES), jnp.float32) for _ in range(HALVES)]
        for s, q, col in chunks(source):
            for h in range(HALVES):
                u = inside(rows[h], col)
                u2 = u * u
                heavy = u2 * col[3]
                weights[t, h, pl.ds(s * LANES + q, CHUNK), :] = heavy * u
                total[h] = total[h] + (heavy * u2) * (1.25 - u)
        for h in range(HALVES):
            value = jnp.sum(total[h], axis=0, keepdims=True)
            inv = rows[h][3]
            parts[own, pl.ds(t * HALVES + h, 1), :] = value * (inv * inv * inv) * (4.0 * DENSITY_SCALE)
    each(start(parts, parts_sem))

    def prepare(t, carry):
        rows, source = task(t)
        total = [[jnp.zeros((CHUNK, LANES), jnp.float32) for _ in range(3)] for _ in range(HALVES)]
        for s, q, col in chunks(source):
            for h in range(HALVES):
                weight = weights[t, h, pl.ds(s * LANES + q, CHUNK), :]
                for d in range(3):
                    term = weight * (rows[h][d] - col[d])
                    waiting[t, d * HALVES + h, pl.ds(s * LANES + q, CHUNK), :] = term
                    total[h][d] = total[h][d] + term
        for h in range(HALVES):
            inv = rows[h][3]
            fifth = FORCE_SCALE * (inv * inv) * (inv * inv) * inv
            early[t, pl.ds(3 * HALVES + h, 1), :] = jnp.where(rows[h][4] > 0.0, fifth, 0.0)
            for d in range(3):
                early[t, pl.ds(d * HALVES + h, 1), :] = jnp.sum(total[h][d], axis=0, keepdims=True)
        return carry

    lax.fori_loop(0, pairs, prepare, 0)

    whole(tail, far_sem, 2 * groups).wait_recv()
    for slot in range(3 * groups):
        for c in range(cells):
            m = pool[slot, c, pl.ds(3 * HALVES, HALVES), :]
            inv = 1.0 / tail[slot, pl.ds(c * HALVES, HALVES), :]
            rho[pl.ds((slot * cells + c) * HALVES, HALVES), :] = m * (inv * inv * inv) * DENSITY_SCALE

    whole(parts, parts_sem, around - 1).wait_recv()

    span = slab_cells * HALVES
    index = lax.broadcasted_iota(jnp.int32, (span, LANES), 0)
    odd = lax.rem(index, HALVES)
    cell_of = (index // HALVES).astype(jnp.float32)
    for d in range(3):
        total = rho[pl.ds(d * span, span), :]
        for g in range(groups):
            slot = d * groups + g
            part = parts[slot]
            to = tail[slot]
            for t in range(pairs):
                value = part[t * HALVES:t * HALVES + 1]
                for h in range(1, HALVES):
                    value = jnp.where(odd == h, part[t * HALVES + h:t * HALVES + h + 1], value)
                at = to[cells * HALVES + t:cells * HALVES + t + 1]
                total = total + jnp.where(cell_of == at, value, 0.0)
        rho[pl.ds(d * span, span), :] = total

    source_rho = [rho[pl.ds(tasks_ref[1, t] * HALVES, HALVES), :] for t in range(pairs)]
    source_rho = 1.0 / jnp.maximum(jnp.concatenate(source_rho, axis=0), 1e-30)
    columns = jnp.transpose(source_rho)
    to_cell = [None] * slab_cells
    for t in range(pairs):
        recv = tasks_ref[0, t]
        a_rho = 1.0 / jnp.maximum(rho[pl.ds((slab_cells + recv) * HALVES, HALVES), :], 1e-30)
        total = [[jnp.zeros((CHUNK, LANES), jnp.float32) for _ in range(3)] for _ in range(HALVES)]
        for s in range(HALVES):
            for q in range(0, LANES, CHUNK):
                col = columns[q:q + CHUNK, t * HALVES + s:t * HALVES + s + 1]
                for h in range(HALVES):
                    for d in range(3):
                        term = waiting[t, d * HALVES + h, pl.ds(s * LANES + q, CHUNK), :]
                        total[h][d] = total[h][d] + term * col
        sums = []
        for d in range(3):
            for h in range(HALVES):
                at = pl.ds(d * HALVES + h, 1)
                value = jnp.sum(total[h][d], axis=0, keepdims=True) + early[t, at, :] * a_rho[h:h + 1]
                sums.append(value * early[t, pl.ds(3 * HALVES + h, 1), :])
        sums = jnp.concatenate(sums, axis=0)
        for cell in range(slab_cells):
            value = jnp.where(recv == cell, sums, 0.0)
            to_cell[cell] = value if t == 0 else to_cell[cell] + value

    rows = 3 * HALVES
    for cell in range(slab_cells):
        to_owner[cell // cells, pl.ds(cell % cells * rows, rows), :] = to_cell[cell]

    def owner_copy(e, z, n):
        pltpu.make_async_remote_copy(
            src_ref=to_owner.at[z], dst_ref=forces.at[member], send_sem=force_sem.at[0], recv_sem=force_sem.at[1],
            device_id=place(0, z), device_id_type=MESH,
        ).start()

    each_near(owner_copy)

    for c in range(cells):
        for h in range(HALVES):
            live = (lane + h * LANES < counts_ref[c]).astype(jnp.float32)
            rho_own[pl.ds(c * HALVES + h, 1), :] = rho[pl.ds((own * cells + c) * HALVES + h, 1), :] * live
    outs = [
        pltpu.make_async_copy(to_owner.at[member], forces.at[member], in_sem.at[0]),
        pltpu.make_async_copy(rho_own, rho_out, in_sem.at[1]),
    ]
    for copy in outs:
        copy.start()

    whole(pool, main_sem, around - 1).wait_send()
    whole(tail, near_sem, groups - 1).wait_send()
    whole(tail, far_sem, 2 * groups).wait_send()
    whole(parts, parts_sem, around - 1).wait_send()
    for copy in outs:
        copy.wait()
    whole(forces, force_sem, groups - 1).wait_recv()
    whole(to_owner, force_sem, groups - 1).wait_send()


def deliver(density_hbm, forces_hbm, density_out, accel_out, density, forces, accel, sems):
    ins = [
        pltpu.make_async_copy(density_hbm, density, sems.at[0]),
        pltpu.make_async_copy(forces_hbm, forces, sems.at[1]),
    ]
    for copy in ins:
        copy.start()
    ins[0].wait()
    outs = [pltpu.make_async_copy(density, density_out, sems.at[2])]
    outs[0].start()
    ins[1].wait()
    total = forces[0]
    for g in range(1, forces.shape[0]):
        total = total + forces[g]
    for at in range(total.shape[0]):
        c, d, h = at // (3 * HALVES), at // HALVES % 3, at % HALVES
        accel[pl.ds(d, 1), pl.ds(c * CELL + h * LANES, LANES)] = total[at:at + 1]
    outs.append(pltpu.make_async_copy(accel, accel_out, sems.at[3]))
    outs[1].start()
    for copy in outs:
        copy.wait()


def local(positions, mass, smooth, counts, tasks):
    groups, doms = lax.axis_size("grp"), lax.axis_size("dom")
    cells, pairs = counts.shape[0], tasks.shape[1]
    around = 3 * groups
    last = max(8, -(-(cells * HALVES + pairs) // 8) * 8)
    hbm = pl.BlockSpec(memory_space=pltpu.HBM)
    density, forces = pl.pallas_call(
        functools.partial(kernel, doms, groups, cells, pairs),
        out_shape=(
            jax.ShapeDtypeStruct((cells * HALVES, LANES), jnp.float32),
            jax.ShapeDtypeStruct((groups, cells * 3 * HALVES, LANES), jnp.float32),
        ),
        in_specs=[hbm] * 5,
        out_specs=(hbm, hbm),
        scratch_shapes=[
            pltpu.SMEM(tasks.shape, jnp.int32),
            pltpu.SMEM(counts.shape, jnp.int32),
            pltpu.VMEM(positions.shape, jnp.float32),
            pltpu.VMEM((1, mass.shape[0]), jnp.float32),
            pltpu.VMEM((1, smooth.shape[0]), jnp.float32),
            pltpu.VMEM((around, cells, 4 * HALVES, LANES), jnp.float32),
            pltpu.VMEM((around, last, LANES), jnp.float32),
            pltpu.VMEM((groups, last, LANES), jnp.float32),
            pltpu.VMEM((around, pairs * HALVES, LANES), jnp.float32),
            pltpu.VMEM((around * cells * HALVES, LANES), jnp.float32),
            pltpu.VMEM((groups, cells * 3 * HALVES, LANES), jnp.float32),
            pltpu.VMEM((cells * HALVES, LANES), jnp.float32),
            pltpu.VMEM((pairs, HALVES, CELL, LANES), jnp.float32),
            pltpu.VMEM((pairs, 3 * HALVES, CELL, LANES), jnp.float32),
            pltpu.VMEM((pairs, 4 * HALVES, LANES), jnp.float32),
            pltpu.SemaphoreType.DMA((5,)),
            pltpu.SemaphoreType.DMA((2,)),
            pltpu.SemaphoreType.DMA((2,)),
            pltpu.SemaphoreType.DMA((2,)),
            pltpu.SemaphoreType.DMA((2,)),
            pltpu.SemaphoreType.DMA((2,)),
        ],
        compiler_params=pltpu.CompilerParams(
            collective_id=0, has_side_effects=True, vmem_limit_bytes=64 * 1024 * 1024
        ),
    )(tasks, counts, positions, mass[None], smooth[None])
    return pl.pallas_call(
        deliver,
        out_shape=(
            jax.ShapeDtypeStruct(mass.shape, jnp.float32),
            jax.ShapeDtypeStruct(positions.shape, jnp.float32),
        ),
        in_specs=[hbm] * 2,
        out_specs=(hbm, hbm),
        scratch_shapes=[
            pltpu.VMEM(mass.shape, jnp.float32),
            pltpu.VMEM(forces.shape, jnp.float32),
            pltpu.VMEM(positions.shape, jnp.float32),
            pltpu.SemaphoreType.DMA((4,)),
        ],
        compiler_params=pltpu.CompilerParams(vmem_limit_bytes=64 * 1024 * 1024),
    )(density.reshape(-1), forces)


def solution(mesh):
    in_specs = (
        P(None, ("dom", "grp")),
        P(("dom", "grp")),
        P(("dom", "grp")),
        P(("dom", "grp")),
        P(None, ("dom", "grp")),
    )
    out_specs = (P(("dom", "grp")), P(None, ("dom", "grp")))
    return jax.shard_map(local, mesh=mesh, in_specs=in_specs, out_specs=out_specs, check_vma=False)
```
